512 devices in a mesh: phys: 2 (over core), sta: 64 (over z, y), cell: 4 (over x).
Axes of the slice: x: 4, y: 8, z: 8, core: 2. Of those that a mesh axis runs over, the one named last changes fastest.
Arguments:
- sensitivity: float32 [2, 1024, 131072], P('phys', 'sta', 'cell'), may hold values from -60 to 60, as said below
- observed: float32 [2, 1024], P('phys', 'sta'), may hold values from -6 to 6
- data_weight: float32 [2, 1024], P('phys', 'sta'), may hold values from 0.3 to 3
- phys_weight: float32 [2], P('phys'), may hold values from 0.5 to 2
- start_model: float32 [131072], P('cell'), may hold values from -6 to 6
Outputs:
- cell_weight: float32 [4, 32768], P('cell', 'sta')
- gradient: float32 [4, 32768], P('cell', 'sta')
- final_model: float32 [4, 32768], P('cell', 'sta')
The draws below stay inside these ranges and needn't reach their ends.
Inputs may be any that keep to these rules, and one draw needn't show every extreme that they name: `sensitivity`: dense, full rank sensitivities.
All inputs are finite; a program needn't handle non-finite values.
Results may differ from the reference program's by a relative error of at most 0.0003.
Values sent between devices are 32-bit elements; how exact they have to be, the bound alone decides.
No kernel may reach another device: no remote copies, remote signals or barrier semaphores. Data moves between devices by JAX's collectives and lax.ppermute only.
A program may use at most 64 MiB of HBM per device.

```python
import math
import jax
import jax.numpy as jnp
from jax import lax

CELL_DEV = 32768
ITERS = 2
PHYSICS = 2
STATIONS = 1024
CELLS = 131072


def draw_sensitivity(key, part):
    key = jax.random.fold_in(key, 11)
    key_noise, key_rows, key_cols = jax.random.split(key, 3)
    row_scale = jnp.exp(jax.random.uniform(key_rows, (PHYSICS, STATIONS, 1), jnp.float32, math.log(0.3), math.log(3.0)))
    col_scale = jnp.exp(jax.random.uniform(key_cols, (1, 1, CELLS), jnp.float32, math.log(0.3), math.log(3.0)))
    noise = jnp.clip(jax.random.normal(key_noise, (PHYSICS, STATIONS, CELLS), jnp.float32), -6.0, 6.0)
    values = noise * row_scale * col_scale
    return values.astype(jnp.float32)


def level_of(key, shape, shards, smallest, largest):
    gain, own = 1.0, jax.random.fold_in(key, 6)
    for axis_at, shards_of in shards:
        steps = jnp.exp(jax.random.uniform(jax.random.fold_in(own, axis_at), (shards_of,), jnp.float32, smallest / len(shards), largest / len(shards)))
        gain = gain * jnp.repeat(steps, shape[axis_at] // shards_of).reshape([-1 if axis == axis_at else 1 for axis in range(len(shape))])
    return gain


def bell_draw(rng, extent, scale, most, pieces=(), held_as=jnp.bfloat16):
    array = scale * jax.random.normal(rng, extent, jnp.float32)
    if pieces:
        array = array * level_of(rng, extent, pieces, -0.22, 0.18)
    return jnp.clip(array, -most, most).astype(held_as)


def setup_inputs(seed: int = 0) -> dict:
    seeds = jax.random.split(jax.random.key(seed), 6)
    return {
        "sensitivity": draw_sensitivity(jax.random.fold_in(seeds[5], 71), 0),
        "observed": bell_draw(seeds[1], (PHYSICS, STATIONS), 1.0, 6.0, ((0, 2), (1, 64)), jnp.float32),
        "data_weight": jnp.clip(jnp.exp(math.log(3.0) - 2.3025851 * jax.random.uniform(seeds[2], (PHYSICS, STATIONS), jnp.float32) ** level_of(seeds[2], (PHYSICS, STATIONS), ((0, 2), (1, 64)), -0.2, 0.2)), 0.3, 3.0),
        "phys_weight": jnp.clip(jnp.exp(math.log(2.0) - 1.3862944 * jax.random.uniform(seeds[3], (PHYSICS,), jnp.float32) ** level_of(seeds[3], (PHYSICS,), ((0, 2),), -0.2, 0.2)), 0.5, 2.0),
        "start_model": bell_draw(seeds[4], (CELLS,), 1.0, 6.0, ((0, 4),), jnp.float32),
    }


step_size = 0.5
weight_floor = 0.1
epsilon = 1e-06

def reference(sensitivity, observed, data_weight, phys_weight, start_model):
    highest = lax.Precision.HIGHEST
    weight_sq = data_weight * data_weight

    def column_of(pair):
        sens_block, weights = pair
        return jnp.dot(weights, sens_block * sens_block, precision=highest)
    column = lax.map(column_of, (sensitivity, weight_sq))
    column_max = lax.optimization_barrier(jnp.max(column, axis=1))
    relative = jnp.sqrt(column / (column_max[:, None] + epsilon))
    weight_flat = weight_floor + lax.optimization_barrier(jnp.sum(relative, axis=0)) / PHYSICS
    model_now = start_model
    gradient_now = jnp.zeros_like(start_model)
    for step_index in range(ITERS):
        predicted = lax.map(lambda sens_block: jnp.dot(sens_block, model_now, precision=highest), sensitivity)
        predicted = predicted / math.sqrt(CELLS)
        residual = data_weight * (predicted - observed)
        weighted = phys_weight[:, None] * data_weight * residual
        terms = lax.map(lambda pair: jnp.dot(pair[0], pair[1], precision=highest), (weighted, sensitivity))
        summed = lax.optimization_barrier(jnp.sum(terms, axis=0))
        gradient_now = summed / (math.sqrt(STATIONS) * weight_flat)
        model_now = model_now - step_size * gradient_now
    shape_out = (CELLS // CELL_DEV, CELL_DEV)
    return (weight_flat.reshape(shape_out), gradient_now.reshape(shape_out), model_now.reshape(shape_out))
```

```python
import math

import jax
import jax.numpy as jnp
from jax import lax
from jax.sharding import PartitionSpec as P

ITERS = 2
LANES = 128

step_size = 0.5
weight_floor = 0.1
epsilon = 1e-06


def per_device(sensitivity, observed, data_weight, phys_weight, start_model):
    highest = lax.Precision.HIGHEST
    sta_count = lax.axis_size("sta")
    cell_blocks = lax.axis_size("cell")
    phys_count = lax.axis_size("phys")
    cell_count = sensitivity.shape[2]
    rows = cell_count // sta_count // LANES
    physics = sensitivity.shape[0] * phys_count
    root_cells = math.sqrt(cell_count * cell_blocks)
    root_stations = math.sqrt(sensitivity.shape[1] * sta_count)
    sens = sensitivity[0]
    weight_sq = data_weight * data_weight
    position = lax.axis_index("sta")
    cell_at = lax.axis_index("cell")

    def slices(vector):
        return vector.reshape(sta_count, rows, LANES)

    def gradient_terms(local_pred):
        predicted = lax.psum(local_pred, "cell") / root_cells
        residual = data_weight * (predicted - observed)
        weighted = phys_weight[:, None] * data_weight * residual
        return slices(jnp.einsum("sc,ps->pc", sens, weighted, precision=highest))

    def to_owners(terms):
        return jnp.sum(lax.all_to_all(terms, "sta", 0, 0, tiled=True), axis=0)

    column_terms = slices(jnp.einsum("ps,sc->pc", weight_sq, sens * sens, precision=highest))
    first_terms = gradient_terms(jnp.einsum("sc,c->s", sens, start_model, precision=highest)[None])
    own = to_owners(jnp.concatenate([column_terms, first_terms], axis=1))
    both = lax.all_to_all(
        jnp.broadcast_to(own[None], (phys_count * cell_blocks,) + own.shape), ("phys", "cell"), 0, 0, tiled=True
    ).reshape(phys_count, cell_blocks, 2 * rows, LANES)
    slice_max = jnp.max(both[:, :, :rows], axis=(1, 2, 3))
    mine = lax.dynamic_index_in_dim(both, cell_at, axis=1, keepdims=False)
    message = jnp.concatenate(
        [
            mine[:, :rows].reshape(phys_count * rows, LANES),
            jnp.sum(mine[:, rows:], axis=0),
            jnp.broadcast_to(slice_max[:, None], (phys_count, LANES)),
        ],
        axis=0,
    )
    message = jnp.pad(message, ((0, 16 - message.shape[0]), (0, 0)))
    gathered = lax.all_to_all(
        jnp.broadcast_to(message[None], (sta_count,) + message.shape), "sta", 0, 0, tiled=True
    )
    column = gathered[:, : phys_count * rows].reshape(sta_count, phys_count, rows, LANES)
    first_summed = gathered[:, phys_count * rows : (phys_count + 1) * rows]
    max_at = (phys_count + 1) * rows
    column_max = jnp.max(gathered[:, max_at : max_at + phys_count], axis=(0, 2))
    relative = jnp.sqrt(column / (column_max[None, :, None, None] + epsilon))
    weight = weight_floor + jnp.sum(relative, axis=1) / physics
    model = slices(start_model) - step_size * (first_summed / (root_stations * weight))

    second_terms = gradient_terms(jnp.einsum("sc,c->s", sens, model.reshape(cell_count), precision=highest)[None])
    second = to_owners(second_terms)
    second_summed = jnp.sum(lax.all_gather(second, "phys"), axis=0)
    weight_own = lax.dynamic_index_in_dim(weight, position, keepdims=False)
    model_own = lax.dynamic_index_in_dim(model, position, keepdims=False)
    gradient = second_summed / (root_stations * weight_own)
    final = model_own - step_size * gradient
    return weight_own.reshape(1, -1), gradient.reshape(1, -1), final.reshape(1, -1)


def solution(mesh):
    return jax.shard_map(
        per_device,
        mesh=mesh,
        in_specs=(
            P("phys", "sta", "cell"),
            P("phys", "sta"),
            P("phys", "sta"),
            P("phys"),
            P("cell"),
        ),
        out_specs=(P("cell", "sta"), P("cell", "sta"), P("cell", "sta")),
        check_vma=False,
    )
```

```python
import functools
import math

import jax
import jax.numpy as jnp
from jax import lax
from jax.experimental import pallas as pl
from jax.experimental.pallas import tpu as pltpu
from jax.sharding import PartitionSpec as P

ITERS = 2
LANES = 128
SUB = 8

step_size = 0.5
weight_floor = 0.1
epsilon = 1e-06

VMEM = pl.BlockSpec(memory_space=pltpu.VMEM)


def chunk(sens, half, at):
    return sens[half * SUB : (half + 1) * SUB, pl.ds(at * LANES, LANES)]


def predict(sens, model, halves):
    chunks = model.shape[0]

    def body(step, acc):
        acc = list(acc)
        for k in range(SUB):
            at = step * SUB + k
            row = model[pl.ds(at, 1), :]
            for half in range(halves):
                slot = (k % 4) * halves + half
                acc[slot] = acc[slot] + chunk(sens, half, at) * row
        return tuple(acc)

    zero = jnp.zeros((SUB, LANES), jnp.float32)
    acc = lax.fori_loop(0, chunks // SUB, body, (zero,) * (4 * halves), unroll=2)
    return [
        (acc[half] + acc[halves + half]) + (acc[2 * halves + half] + acc[3 * halves + half])
        for half in range(halves)
    ]


def as_column(row, halves):
    stations = SUB * halves
    wide = jnp.broadcast_to(row, (stations, stations))
    at = lax.broadcasted_iota(jnp.int32, (stations, stations), 0)
    to = lax.broadcasted_iota(jnp.int32, (stations, stations), 1)
    column = jnp.sum(jnp.where(at == to, wide, 0.0), axis=1, keepdims=True)
    return [column[half * SUB : (half + 1) * SUB] for half in range(halves)]


def weighted_residual(parts, observed, data_weight, phys_weight, halves, root_cells):
    total = parts[0]
    for block in range(1, parts.shape[0]):
        total = total + parts[block]
    predicted = jnp.sum(total, axis=1, keepdims=True) / root_cells
    seen = as_column(observed[...], halves)
    weight = as_column(data_weight[...], halves)
    scale = phys_weight[0, 0]
    weighted = []
    for half in range(halves):
        residual = weight[half] * (predicted[half * SUB : (half + 1) * SUB] - seen[half])
        weighted.append(scale * weight[half] * residual)
    return weight, weighted


def predict_kernel(sens, model, out):
    halves = sens.shape[0] // SUB
    acc = predict(sens, model, halves)
    for block in range(out.shape[0]):
        for half in range(halves):
            out[block, half * SUB : (half + 1) * SUB, :] = acc[half]


def first_terms_kernel(root_cells, parts, sens, observed, data_weight, phys_weight, out):
    halves = sens.shape[0] // SUB
    rows = out.shape[1] // 2
    weight, weighted = weighted_residual(parts, observed, data_weight, phys_weight, halves, root_cells)
    wide = [jnp.broadcast_to(w, (SUB, LANES)) for w in weighted]
    square = [jnp.broadcast_to(w * w, (SUB, LANES)) for w in weight]

    def body(owner, carry):
        for row in range(rows):
            column = gradient = None
            for half in range(halves):
                block = chunk(sens, half, owner * rows + row)
                c = block * block * square[half]
                g = block * wide[half]
                column = c if column is None else column + c
                gradient = g if gradient is None else gradient + g
            out[owner, row : row + 1, :] = jnp.sum(column, axis=0, keepdims=True)
            out[owner, rows + row : rows + row + 1, :] = jnp.sum(gradient, axis=0, keepdims=True)
        return carry

    lax.fori_loop(0, out.shape[0], body, 0, unroll=2)


def second_terms_kernel(root_cells, parts, sens, observed, data_weight, phys_weight, out):
    halves = sens.shape[0] // SUB
    rows = out.shape[1]
    _, weighted = weighted_residual(parts, observed, data_weight, phys_weight, halves, root_cells)
    wide = [jnp.broadcast_to(w, (SUB, LANES)) for w in weighted]

    def body(owner, carry):
        for row in range(rows):
            gradient = None
            for half in range(halves):
                g = chunk(sens, half, owner * rows + row) * wide[half]
                gradient = g if gradient is None else gradient + g
            out[owner, row : row + 1, :] = jnp.sum(gradient, axis=0, keepdims=True)
        return carry

    lax.fori_loop(0, out.shape[0], body, 0, unroll=4)


def sum_leading(ref):
    return jnp.sum(ref[...], axis=0)


def owner_sum_kernel(received, out):
    total = sum_leading(received)
    for peer in range(out.shape[0]):
        out[peer] = total


def message_kernel(rows, cell_blocks, both, out):
    phys_count = both.shape[0] // cell_blocks
    cell_at = lax.axis_index("cell")
    gradient = None
    pieces, largest = [], []
    for method in range(phys_count):
        block = both[method * cell_blocks + cell_at]
        pieces.append(block[:rows])
        gradient = block[rows:] if gradient is None else gradient + block[rows:]
        most = both[method * cell_blocks, :rows]
        for other in range(1, cell_blocks):
            most = jnp.maximum(most, both[method * cell_blocks + other, :rows])
        largest.append(jnp.max(most, axis=0, keepdims=True))
    used = rows * (phys_count + 1) + phys_count
    fill = jnp.zeros((out.shape[1] - used, LANES), jnp.float32)
    tile = jnp.concatenate(pieces + [gradient] + largest + [fill], axis=0)

    def body(peer, carry):
        out[peer] = tile
        return carry

    lax.fori_loop(0, out.shape[0], body, 0, unroll=8)


def model_kernel(rows, phys_count, physics, root_stations, message, start, sens, parts, own, model):
    owners = message.shape[0]
    position = lax.axis_index("sta")
    max_at = rows * (phys_count + 1)
    most = jnp.max(message[:, max_at : max_at + phys_count, :], axis=0)
    most = jnp.max(most, axis=1, keepdims=True)
    scales = 1.0 / (most + epsilon)

    def weights(owner):
        relative = None
        for method in range(phys_count):
            column = message[owner, method * rows : (method + 1) * rows, :]
            r = jnp.sqrt(column * scales[method : method + 1])
            relative = r if relative is None else relative + r
        return weight_floor + relative / physics

    def stepped(owner, weight):
        summed = message[owner, phys_count * rows : (phys_count + 1) * rows, :]
        return start[owner] - step_size * (summed / (root_stations * weight))

    def body(owner, carry):
        model[pl.ds(owner * rows, rows), :] = stepped(owner, weights(owner))
        return carry

    lax.fori_loop(0, owners, body, 0, unroll=4)
    weight_own = weights(position)
    own[0] = weight_own
    own[1] = stepped(position, weight_own)
    halves = sens.shape[0] // SUB
    acc = predict(sens, model, halves)
    for block in range(parts.shape[0]):
        for half in range(halves):
            parts[block, half * SUB : (half + 1) * SUB, :] = acc[half]


def second_sum_kernel(received, out):
    out[...] = sum_leading(received)


def final_kernel(root_stations, summed, own, weight_out, gradient_out, model_out):
    total = sum_leading(summed)
    weight = own[0]
    gradient = total / (root_stations * weight)
    model = own[1] - step_size * gradient
    for row in range(total.shape[0]):
        lanes = slice(row * LANES, (row + 1) * LANES)
        weight_out[:, lanes] = weight[row : row + 1]
        gradient_out[:, lanes] = gradient[row : row + 1]
        model_out[:, lanes] = model[row : row + 1]


def kernel_call(kernel, name, outs, operands, scratch=(), flops=0):
    out_shape = [jax.ShapeDtypeStruct(s, jnp.float32) for s in outs]
    return pl.pallas_call(
        kernel,
        name=name,
        out_shape=out_shape,
        in_specs=[VMEM] * len(operands),
        out_specs=[VMEM] * len(outs),
        scratch_shapes=scratch,
        compiler_params=pltpu.CompilerParams(vmem_limit_bytes=16 * 2**20),
    )(*operands)


def per_device(sensitivity, observed, data_weight, phys_weight, start_model):
    sta_count = lax.axis_size("sta")
    cell_blocks = lax.axis_size("cell")
    phys_count = lax.axis_size("phys")
    stations, cell_count = sensitivity.shape[1:]
    rows = cell_count // sta_count // LANES
    physics = sensitivity.shape[0] * phys_count
    root_cells = math.sqrt(cell_count * cell_blocks)
    root_stations = math.sqrt(stations * sta_count)
    sens = sensitivity.reshape(stations, cell_count)
    start_rows = start_model.reshape(cell_count // LANES, LANES)
    start_slices = start_model.reshape(sta_count, rows, LANES)
    scale = phys_weight.reshape(1, 1)
    message_rows = -(-(rows * (phys_count + 1) + phys_count) // SUB) * SUB

    def swap(array, axes):
        return lax.all_to_all(array, axes, 0, 0, tiled=True)

    parts_shape = (cell_blocks, stations, LANES)
    (parts,) = kernel_call(predict_kernel, "predict", [parts_shape], [sens, start_rows])
    parts = swap(parts, "cell")
    (terms,) = kernel_call(
        functools.partial(first_terms_kernel, root_cells),
        "first_terms",
        [(sta_count, 2 * rows, LANES)],
        [parts, sens, observed, data_weight, scale],
    )
    terms = swap(terms, "sta")
    peers = phys_count * cell_blocks
    (both,) = kernel_call(owner_sum_kernel, "owner_sum", [(peers, 2 * rows, LANES)], [terms])
    both = swap(both, ("phys", "cell"))
    (message,) = kernel_call(
        functools.partial(message_kernel, rows, cell_blocks),
        "message",
        [(sta_count, message_rows, LANES)],
        [both],
    )
    message = swap(message, "sta")
    parts, own = kernel_call(
        functools.partial(model_kernel, rows, phys_count, physics, root_stations),
        "model",
        [parts_shape, (2, rows, LANES)],
        [message, start_slices, sens],
        scratch=[pltpu.VMEM((cell_count // LANES, LANES), jnp.float32)],
    )
    parts = swap(parts, "cell")
    (terms,) = kernel_call(
        functools.partial(second_terms_kernel, root_cells),
        "second_terms",
        [(sta_count, rows, LANES)],
        [parts, sens, observed, data_weight, scale],
    )
    terms = swap(terms, "sta")
    (summed,) = kernel_call(second_sum_kernel, "second_sum", [(rows, LANES)], [terms])
    summed = lax.all_gather(summed, "phys")
    out = (1, rows * LANES)
    return tuple(kernel_call(functools.partial(final_kernel, root_stations), "final", [out] * 3, [summed, own]))


def solution(mesh):
    return jax.shard_map(
        per_device,
        mesh=mesh,
        in_specs=(
            P("phys", "sta", "cell"),
            P("phys", "sta"),
            P("phys", "sta"),
            P("phys"),
            P("cell"),
        ),
        out_specs=(P("cell", "sta"), P("cell", "sta"), P("cell", "sta")),
        check_vma=False,
    )
```

```python
import functools
import math

import jax
import jax.numpy as jnp
from jax import lax
from jax.experimental import pallas as pl
from jax.experimental.pallas import tpu as pltpu
from jax.sharding import PartitionSpec as P

ITERS = 2
LANES = 128
SUB = 8

step_size = 0.5
weight_floor = 0.1
epsilon = 1e-06

def chunk(sens, half, at):
    return sens[half * SUB : (half + 1) * SUB, pl.ds(at * LANES, LANES)]


def predict(sens, model, halves, first, count, acc):
    def body(step, acc):
        acc = list(acc)
        for k in range(SUB):
            at = first + step * SUB + k
            row = model[pl.ds(at, 1), :]
            for half in range(halves):
                slot = (k % 4) * halves + half
                acc[slot] = acc[slot] + chunk(sens, half, at) * row
        return tuple(acc)

    return lax.fori_loop(0, count // SUB, body, acc, unroll=2)


def predict_start(halves):
    return (jnp.zeros((SUB, LANES), jnp.float32),) * (4 * halves)


def predict_store(acc, halves, out):
    for half in range(halves):
        total = (acc[half] + acc[halves + half]) + (acc[2 * halves + half] + acc[3 * halves + half])
        for block in range(out.shape[0]):
            out[block, half * SUB : (half + 1) * SUB, :] = total


def as_column(row):
    stations = row.shape[1]
    wide = jnp.broadcast_to(row, (stations, stations))
    at = lax.broadcasted_iota(jnp.int32, (stations, stations), 0)
    to = lax.broadcasted_iota(jnp.int32, (stations, stations), 1)
    column = jnp.sum(jnp.where(at == to, wide, 0.0), axis=1, keepdims=True)
    return jnp.broadcast_to(column, (stations, LANES))


def weighted_residual(parts, station, root_cells):
    total = parts[0]
    for block in range(1, parts.shape[0]):
        total = total + parts[block]
    predicted = jnp.sum(total, axis=1, keepdims=True) / root_cells
    weight, observed, scaled = station[0], station[1], station[2]
    residual = weight * (predicted - observed)
    return weight, scaled * residual


def predict_kernel(
    sens_hbm, model_hbm, observed_hbm, weight_hbm, scale, out, sens, station, model, observed, weight, sems
):
    halves, pieces = sens.shape[0] // SUB, sems.shape[0] - 3
    size = sens.shape[1] // pieces
    small = [
        pltpu.make_async_copy(source, target, sems.at[pieces + at])
        for at, (source, target) in enumerate(
            [(model_hbm, model), (observed_hbm, observed), (weight_hbm, weight)]
        )
    ]
    large = []
    for piece in range(pieces):
        lanes = pl.ds(piece * size, size)
        large.append(pltpu.make_async_copy(sens_hbm.at[:, lanes], sens.at[:, lanes], sems.at[piece]))
    small[0].start()
    for copy in large:
        copy.start()
    for copy in small[1:]:
        copy.start()
    small[0].wait()
    acc = predict_start(halves)
    for piece in range(pieces):
        large[piece].wait()
        chunks = size // LANES
        acc = predict(sens, model, halves, piece * chunks, chunks, acc)
    predict_store(acc, halves, out)
    for copy in small[1:]:
        copy.wait()
    wide = as_column(weight[...])
    station[0] = wide
    station[1] = as_column(observed[...])
    station[2] = scale[0] * wide


def first_terms_kernel(root_cells, parts, sens, station, out):
    halves = sens.shape[0] // SUB
    rows = out.shape[1] // 2
    weight, wide = weighted_residual(parts, station, root_cells)
    square = weight * weight

    def body(owner, carry):
        for row in range(rows):
            column = gradient = None
            for half in range(halves):
                block = chunk(sens, half, owner * rows + row)
                at = slice(half * SUB, (half + 1) * SUB)
                c = block * block * square[at]
                g = block * wide[at]
                column = c if column is None else column + c
                gradient = g if gradient is None else gradient + g
            out[owner, row : row + 1, :] = jnp.sum(column, axis=0, keepdims=True)
            out[owner, rows + row : rows + row + 1, :] = jnp.sum(gradient, axis=0, keepdims=True)
        return carry

    lax.fori_loop(0, out.shape[0], body, 0, unroll=2)


def second_terms_kernel(root_cells, parts, sens, station, out):
    halves = sens.shape[0] // SUB
    rows = out.shape[1]
    _, wide = weighted_residual(parts, station, root_cells)

    def body(owner, carry):
        for row in range(rows):
            gradient = None
            for half in range(halves):
                g = chunk(sens, half, owner * rows + row) * wide[half * SUB : (half + 1) * SUB]
                gradient = g if gradient is None else gradient + g
            out[owner, row : row + 1, :] = jnp.sum(gradient, axis=0, keepdims=True)
        return carry

    lax.fori_loop(0, out.shape[0], body, 0, unroll=4)


def sum_leading(ref):
    return jnp.sum(ref[...], axis=0)


def owner_sum_kernel(received, out):
    total = sum_leading(received)
    for peer in range(out.shape[0]):
        out[peer] = total


def message_kernel(rows, cell_blocks, owners, both, out):
    phys_count = both.shape[0] // cell_blocks
    size = out.shape[0] // owners
    cell_at = lax.axis_index("cell")
    part = LANES // phys_count
    lane = lax.broadcasted_iota(jnp.int32, (1, LANES), 1)
    gradient = maxima = None
    pieces = []
    for method in range(phys_count):
        block = both[method * cell_blocks + cell_at]
        pieces.append(block[:rows])
        gradient = block[rows:] if gradient is None else gradient + block[rows:]
        most = both[method * cell_blocks, :rows]
        for other in range(1, cell_blocks):
            most = jnp.maximum(most, both[method * cell_blocks + other, :rows])
        largest = jnp.max(jnp.max(most, axis=0, keepdims=True), axis=1, keepdims=True)
        largest = jnp.broadcast_to(largest, (1, LANES))
        maxima = largest if maxima is None else jnp.where(lane >= method * part, largest, maxima)
    message = jnp.concatenate(pieces + [gradient, maxima], axis=0)
    for row in range(size):
        wide = jnp.broadcast_to(message[row : row + 1], (owners, LANES))
        out[pl.ds(row, owners, stride=size), :] = wide


def model_kernel(rows, owners, phys_count, physics, root_stations, message, start, sens, parts, own, model, weights):
    position = lax.axis_index("sta")
    size = message.shape[0] // owners
    part = LANES // phys_count
    lane = lax.broadcasted_iota(jnp.int32, (1, LANES), 1)
    most = jnp.max(message[pl.ds(size - 1, owners, stride=size), :], axis=0, keepdims=True)
    scales = []
    for method in range(phys_count):
        inside = (lane >= method * part) & (lane < (method + 1) * part)
        largest = jnp.max(jnp.where(inside, most, 0.0), axis=1, keepdims=True)
        scales.append(1.0 / (largest + epsilon))
    for row in range(rows):
        relative = None
        for method in range(phys_count):
            column = message[pl.ds(method * rows + row, owners, stride=size), :]
            r = jnp.sqrt(column * scales[method])
            relative = r if relative is None else relative + r
        weight = weight_floor + relative / physics
        summed = message[pl.ds(phys_count * rows + row, owners, stride=size), :]
        at = pl.ds(row, owners, stride=rows)
        model[at, :] = start[at, :] - step_size * (summed / (root_stations * weight))
        weights[at, :] = weight
    halves = sens.shape[0] // SUB
    acc = predict(sens, model, halves, 0, model.shape[0], predict_start(halves))
    predict_store(acc, halves, parts)
    own_rows = pl.ds(position * rows, rows)
    own[0] = weights[own_rows, :]
    own[1] = model[own_rows, :]


def second_sum_kernel(received, out):
    out[...] = sum_leading(received)


def final_kernel(root_stations, summed, own, weight_out, gradient_out, model_out):
    total = sum_leading(summed)
    weight = own[0]
    gradient = total / (root_stations * weight)
    model = own[1] - step_size * gradient
    for row in range(total.shape[0]):
        lanes = slice(row * LANES, (row + 1) * LANES)
        weight_out[:, lanes] = weight[row : row + 1]
        gradient_out[:, lanes] = gradient[row : row + 1]
        model_out[:, lanes] = model[row : row + 1]


def kernel_call(kernel, name, outs, operands, scratch=(), spaces=None, kept=True):
    spaces = spaces or [pltpu.VMEM] * len(operands)
    operands = [
        pltpu.with_memory_space_constraint(x, space) if space == pltpu.HBM else x for x, space in zip(operands, spaces)
    ]
    make = pltpu.VMEM if kept else jax.ShapeDtypeStruct
    return pl.pallas_call(
        kernel,
        name=name,
        out_shape=[make(shape, jnp.float32) for shape in outs],
        in_specs=[pl.BlockSpec(memory_space=space) for space in spaces],
        out_specs=[pl.BlockSpec(memory_space=pltpu.VMEM)] * len(outs),
        scratch_shapes=scratch,
        compiler_params=pltpu.CompilerParams(vmem_limit_bytes=16 * 2**20),
    )(*operands)


def per_device(sensitivity, observed, data_weight, phys_weight, start_model):
    sta_count = lax.axis_size("sta")
    cell_blocks = lax.axis_size("cell")
    phys_count = lax.axis_size("phys")
    stations, cell_count = sensitivity.shape[1:]
    chunks = cell_count // LANES
    rows = chunks // sta_count
    physics = sensitivity.shape[0] * phys_count
    root_cells = math.sqrt(cell_count * cell_blocks)
    root_stations = math.sqrt(stations * sta_count)
    sens = sensitivity.reshape(stations, cell_count)
    start = start_model.reshape(chunks, LANES)
    size = rows * (phys_count + 1) + 1
    peers = phys_count * cell_blocks
    pieces = 8

    def swap(array, axes):
        return lax.all_to_all(array, axes, 0, 0, tiled=True)

    parts_shape = (cell_blocks, stations, LANES)
    parts, sens, station = kernel_call(
        predict_kernel,
        "predict",
        [parts_shape, (stations, cell_count), (3, stations, LANES)],
        [sens, start, observed, data_weight, phys_weight],
        scratch=[
            pltpu.VMEM((chunks, LANES), jnp.float32),
            pltpu.VMEM((1, stations), jnp.float32),
            pltpu.VMEM((1, stations), jnp.float32),
            pltpu.SemaphoreType.DMA((pieces + 3,)),
        ],
        spaces=[pltpu.HBM] * 4 + [pltpu.SMEM],
    )
    parts = swap(parts, "cell")
    (terms,) = kernel_call(
        functools.partial(first_terms_kernel, root_cells),
        "first_terms",
        [(sta_count, 2 * rows, LANES)],
        [parts, sens, station],
    )
    terms = swap(terms, "sta")
    (both,) = kernel_call(owner_sum_kernel, "owner_sum", [(peers, 2 * rows, LANES)], [terms])
    both = swap(both, ("phys", "cell"))
    (message,) = kernel_call(
        functools.partial(message_kernel, rows, cell_blocks, sta_count),
        "message",
        [(sta_count * size, LANES)],
        [both],
    )
    message = swap(message.reshape(sta_count, 1, size * LANES), "sta").reshape(sta_count * size, LANES)
    parts, own = kernel_call(
        functools.partial(model_kernel, rows, sta_count, phys_count, physics, root_stations),
        "model",
        [parts_shape, (2, rows, LANES)],
        [message, start, sens],
        scratch=[pltpu.VMEM((chunks, LANES), jnp.float32)] * 2,
    )
    parts = swap(parts, "cell")
    (terms,) = kernel_call(
        functools.partial(second_terms_kernel, root_cells),
        "second_terms",
        [(sta_count, rows, LANES)],
        [parts, sens, station],
    )
    terms = swap(terms, "sta")
    (summed,) = kernel_call(second_sum_kernel, "second_sum", [(rows, LANES)], [terms])
    summed = lax.all_gather(summed, "phys")
    out = (1, rows * LANES)
    return tuple(
        kernel_call(functools.partial(final_kernel, root_stations), "final", [out] * 3, [summed, own], kept=False)
    )


def solution(mesh):
    return jax.shard_map(
        per_device,
        mesh=mesh,
        in_specs=(
            P("phys", "sta", "cell"),
            P("phys", "sta"),
            P("phys", "sta"),
            P("phys"),
            P("cell"),
        ),
        out_specs=(P("cell", "sta"), P("cell", "sta"), P("cell", "sta")),
        check_vma=False,
    )
```

```python
import functools
import math

import jax
import jax.numpy as jnp
from jax import lax
from jax.experimental import pallas as pl
from jax.experimental.pallas import tpu as pltpu
from jax.sharding import PartitionSpec as P

ITERS = 2
LANES = 128
SUB = 8

step_size = 0.5
weight_floor = 0.1
epsilon = 1e-06


def lane_index(rows):
    return lax.broadcasted_iota(jnp.int32, (rows, LANES), 1)


def as_column(row):
    stations = row.shape[1]
    wide = jnp.broadcast_to(row, (stations, stations))
    at = lax.broadcasted_iota(jnp.int32, (stations, stations), 0)
    to = lax.broadcasted_iota(jnp.int32, (stations, stations), 1)
    return jnp.sum(jnp.where(at == to, wide, 0.0), axis=1, keepdims=True)


def in_lanes(columns):
    lane = lane_index(columns[0].shape[0])
    tile = jnp.zeros(lane.shape, jnp.float32)
    for at, column in enumerate(columns):
        tile = jnp.where(lane == at, column, tile)
    return tile


def lanes_of(chunk):
    return pl.ds(chunk * LANES, LANES)


def store_row(out, at, value):
    out[pl.ds(at, 1), :] = jnp.sum(value, axis=0, keepdims=True)


def predict_kernel(
    rows, sens_hbm, model_hbm, observed_hbm, weight_hbm, scale, out, sens, send, model, observed, weight, sems
):
    halves, pieces = sens.shape[0] // SUB, sems.shape[0] - 3
    size = sens.shape[1] // pieces
    share = rows // 2
    core = lax.axis_index("phys")
    small = [
        pltpu.make_async_copy(source, target, sems.at[pieces + at])
        for at, (source, target) in enumerate(
            [(model_hbm, model), (observed_hbm, observed), (weight_hbm, weight)]
        )
    ]
    large = []
    for piece in range(pieces):
        lanes = pl.ds(piece * size, size)
        large.append(pltpu.make_async_copy(sens_hbm.at[:, lanes], sens.at[:, lanes], sems.at[piece]))
    small[0].start()
    for copy in large:
        copy.start()
    for copy in small[1:]:
        copy.start()
    small[0].wait()
    owners = size // LANES // rows

    def body(owner, acc):
        acc = list(acc)
        for row in range(rows):
            at = owner * rows + row
            value = model[pl.ds(at, 1), :]
            for half in range(halves):
                slot = (row % 4) * halves + half
                acc[slot] = acc[slot] + sens[half * SUB : (half + 1) * SUB, lanes_of(at)] * value
        for row in range(share):
            source = lanes_of(owner * rows + (1 - core) * share + row)
            send[:, lanes_of(owner * share + row)] = sens[:, source]
        return tuple(acc)

    acc = (jnp.zeros((SUB, LANES), jnp.float32),) * (4 * halves)
    for piece in range(pieces):
        large[piece].wait()
        acc = lax.fori_loop(piece * owners, (piece + 1) * owners, body, acc, unroll=4)
    total = [
        (acc[half] + acc[halves + half]) + (acc[2 * halves + half] + acc[3 * halves + half]) for half in range(halves)
    ]
    part = jnp.sum(jnp.concatenate(total, axis=0), axis=1, keepdims=True)
    for copy in small[1:]:
        copy.wait()
    column = as_column(weight[...])
    tile = in_lanes([part, column, as_column(observed[...]), scale[0] * column])
    for peer in range(out.shape[0]):
        out[peer] = tile


def residual_weights(predicted, station):
    weight, observed, scaled = station[:, 1:2], station[:, 2:3], station[:, 3:4]
    residual = weight * (predicted - observed)
    shape = (station.shape[0], LANES)
    return jnp.broadcast_to(weight, shape), jnp.broadcast_to(scaled * residual, shape)


def first_terms_kernel(rows, owners, cell_blocks, root_cells, parts, sens, got, out):
    halves = sens.shape[0] // SUB
    share = rows // 2
    core = lax.axis_index("phys")
    squares, wides = [], []
    for method in (core, 1 - core):
        station = parts[method * cell_blocks]
        total = station
        for block in range(1, cell_blocks):
            total = total + parts[method * cell_blocks + block]
        weight, wide = residual_weights(total[:, 0:1] / root_cells, station)
        squares.append(weight * weight)
        wides.append(wide)

    def body(owner, carry):
        for row in range(share):
            sources = (
                (sens, lanes_of(owner * rows + core * share + row)),
                (got, lanes_of(owner * share + row)),
            )
            gradient = None
            for method, (source, lanes) in enumerate(sources):
                column = None
                for half in range(halves):
                    at = slice(half * SUB, (half + 1) * SUB)
                    block = source[at, lanes]
                    c = block * block * squares[method][at]
                    g = block * wides[method][at]
                    column = c if column is None else column + c
                    gradient = g if gradient is None else gradient + g
                store_row(out, (owner * 3 + method) * share + row, column)
            store_row(out, (owner * 3 + 2) * share + row, gradient)
        return carry

    lax.fori_loop(0, owners, body, 0, unroll=4)


def owner_sum_kernel(rows, owners, received, own, out):
    share = rows // 2
    core = lax.axis_index("phys")
    size = 3 * share
    for row in range(size):
        own[row : row + 1, :] = jnp.sum(received[pl.ds(row, owners, stride=size), :], axis=0, keepdims=True)
    largest = []
    for method in range(2):
        most = jnp.max(own[method * share : (method + 1) * share, :], axis=0, keepdims=True)
        largest.append(jnp.max(most, axis=1, keepdims=True))
    first = jnp.where(core == 0, largest[0], largest[1])
    second = jnp.where(core == 0, largest[1], largest[0])
    tile = jnp.where(lane_index(1) < LANES // 2, first, second)
    for peer in range(out.shape[0]):
        out[peer] = tile


def message_kernel(owners, maxima, own, out):
    size = own.shape[0] + 1
    most = maxima[0]
    for peer in range(1, maxima.shape[0]):
        most = jnp.maximum(most, maxima[peer])
    for row in range(size):
        value = own[row : row + 1, :] if row < size - 1 else most
        out[pl.ds(row, owners, stride=size), :] = jnp.broadcast_to(value, (owners, LANES))


def model_kernel(rows, owners, physics, root_stations, message, start, sens, got, out, own, model, weights):
    halves = sens.shape[0] // SUB
    share = rows // 2
    core = lax.axis_index("phys")
    position = lax.axis_index("sta")
    size = message.shape[0] // owners
    most = jnp.max(message[pl.ds(size - 1, owners, stride=size), :], axis=0, keepdims=True)
    first_lanes = lane_index(1) < LANES // 2
    scales = []
    for method in (core, 1 - core):
        inside = first_lanes == (method == 0)
        largest = jnp.max(jnp.where(inside, most, 0.0), axis=1, keepdims=True)
        scales.append(1.0 / (largest + epsilon))
    for row in range(share):
        relative = None
        for method in range(2):
            column = message[pl.ds(method * share + row, owners, stride=size), :]
            r = jnp.sqrt(column * scales[method])
            relative = r if relative is None else relative + r
        weight = weight_floor + relative / physics
        summed = message[pl.ds(2 * share + row, owners, stride=size), :]
        before = [start[pl.ds(at * share + row, owners, stride=rows), :] for at in range(2)]
        at = pl.ds(row, owners, stride=share)
        model[at, :] = jnp.where(core == 0, before[0], before[1]) - step_size * (summed / (root_stations * weight))
        weights[at, :] = weight

    def body(owner, acc):
        acc = list(acc)
        for row in range(share):
            value = model[pl.ds(owner * share + row, 1), :]
            sources = (
                (sens, lanes_of(owner * rows + core * share + row)),
                (got, lanes_of(owner * share + row)),
            )
            for method, (source, lanes) in enumerate(sources):
                for half in range(halves):
                    slot = ((row % 2) * 2 + method) * halves + half
                    acc[slot] = acc[slot] + source[half * SUB : (half + 1) * SUB, lanes] * value
        return tuple(acc)

    acc = (jnp.zeros((SUB, LANES), jnp.float32),) * (4 * halves)
    acc = lax.fori_loop(0, owners, body, acc, unroll=4)
    columns = []
    for method in range(2):
        total = [acc[method * halves + half] + acc[(2 + method) * halves + half] for half in range(halves)]
        columns.append(jnp.sum(jnp.concatenate(total, axis=0), axis=1, keepdims=True))
    lane = lane_index(columns[0].shape[0])
    tile = jnp.where(lane == core, columns[0], jnp.where(lane == 1 - core, columns[1], 0.0))
    for peer in range(out.shape[0]):
        out[peer] = tile
    own_rows = pl.ds(position * share, share)
    own[0] = weights[own_rows, :]
    own[1] = model[own_rows, :]


def second_terms_kernel(rows, owners, cell_blocks, root_cells, parts, stations, sens, got, out):
    halves = sens.shape[0] // SUB
    share = rows // 2
    core = lax.axis_index("phys")
    total = parts[0]
    for peer in range(1, parts.shape[0]):
        total = total + parts[peer]
    lane = lane_index(total.shape[0])
    wides = []
    for method in (core, 1 - core):
        predicted = jnp.sum(jnp.where(lane == method, total, 0.0), axis=1, keepdims=True) / root_cells
        wides.append(residual_weights(predicted, stations[method * cell_blocks])[1])

    def body(owner, carry):
        for row in range(share):
            sources = (
                (sens, lanes_of(owner * rows + core * share + row)),
                (got, lanes_of(owner * share + row)),
            )
            gradient = None
            for method, (source, lanes) in enumerate(sources):
                for half in range(halves):
                    at = slice(half * SUB, (half + 1) * SUB)
                    g = source[at, lanes] * wides[method][at]
                    gradient = g if gradient is None else gradient + g
            store_row(out, owner * share + row, gradient)
        return carry

    lax.fori_loop(0, owners, body, 0, unroll=4)


def second_step_kernel(owners, root_stations, received, own, out):
    share = own.shape[1]
    for row in range(share):
        total = jnp.sum(received[pl.ds(row, owners, stride=share), :], axis=0, keepdims=True)
        weight = own[0, row : row + 1, :]
        gradient = total / (root_stations * weight)
        out[row : row + 1, :] = weight
        out[share + row : share + row + 1, :] = gradient
        out[2 * share + row : 2 * share + row + 1, :] = own[1, row : row + 1, :] - step_size * gradient


def layout_kernel(both, *outs):
    share = both.shape[1] // len(outs)
    for at, out in enumerate(outs):
        for core in range(both.shape[0]):
            for row in range(share):
                to = (core * share + row) * LANES
                source = at * share + row
                out[:, to : to + LANES] = both[core, source : source + 1, :]


def kernel_call(kernel, name, outs, operands, scratch=(), spaces=None, kept=True):
    make = pltpu.VMEM if kept else jax.ShapeDtypeStruct
    spaces = spaces or [pltpu.VMEM] * len(operands)
    operands = [
        pltpu.with_memory_space_constraint(x, space) if space == pltpu.HBM else x for x, space in zip(operands, spaces)
    ]
    return pl.pallas_call(
        kernel,
        name=name,
        out_shape=[make(shape, jnp.float32) for shape in outs],
        in_specs=[pl.BlockSpec(memory_space=space) for space in spaces],
        out_specs=[pl.BlockSpec(memory_space=pltpu.VMEM)] * len(outs),
        scratch_shapes=scratch,
        compiler_params=pltpu.CompilerParams(vmem_limit_bytes=16 * 2**20),
    )(*operands)


def per_device(sensitivity, observed, data_weight, phys_weight, start_model):
    owners = lax.axis_size("sta")
    cell_blocks = lax.axis_size("cell")
    physics = sensitivity.shape[0] * lax.axis_size("phys")
    stations, cell_count = sensitivity.shape[1:]
    chunks = cell_count // LANES
    rows = chunks // owners
    share = rows // 2
    root_cells = math.sqrt(cell_count * cell_blocks)
    root_stations = math.sqrt(stations * owners)
    sens = sensitivity.reshape(stations, cell_count)
    start = start_model.reshape(chunks, LANES)
    peers = physics * cell_blocks
    pieces = min(8, owners)

    def swap(array, axes):
        return lax.all_to_all(array, axes, 0, 0, tiled=True)

    def swap_rows(array):
        return swap(array.reshape(owners, 1, -1), "sta").reshape(array.shape)

    parts_shape = (peers, stations, LANES)
    first, sens, send = kernel_call(
        functools.partial(predict_kernel, rows),
        "predict",
        [parts_shape, (stations, cell_count), (stations, cell_count // 2)],
        [sens, start, observed, data_weight, phys_weight],
        scratch=[
            pltpu.VMEM((chunks, LANES), jnp.float32),
            pltpu.VMEM((1, stations), jnp.float32),
            pltpu.VMEM((1, stations), jnp.float32),
            pltpu.SemaphoreType.DMA((pieces + 3,)),
        ],
        spaces=[pltpu.HBM] * 4 + [pltpu.SMEM],
    )
    got = lax.ppermute(send, "phys", [(0, 1), (1, 0)])
    first = swap(first, ("phys", "cell"))
    (terms,) = kernel_call(
        functools.partial(first_terms_kernel, rows, owners, cell_blocks, root_cells),
        "first_terms",
        [(owners * 3 * share, LANES)],
        [first, sens, got],
    )
    own, maxima = kernel_call(
        functools.partial(owner_sum_kernel, rows, owners),
        "owner_sum",
        [(3 * share, LANES), (peers, 1, LANES)],
        [swap_rows(terms)],
    )
    (message,) = kernel_call(
        functools.partial(message_kernel, owners),
        "message",
        [(owners * (3 * share + 1), LANES)],
        [swap(maxima, ("phys", "cell")), own],
    )
    second, own = kernel_call(
        functools.partial(model_kernel, rows, owners, physics, root_stations),
        "model",
        [parts_shape, (2, share, LANES)],
        [swap_rows(message), start, sens, got],
        scratch=[pltpu.VMEM((chunks // 2, LANES), jnp.float32)] * 2,
    )
    (terms,) = kernel_call(
        functools.partial(second_terms_kernel, rows, owners, cell_blocks, root_cells),
        "second_terms",
        [(owners * share, LANES)],
        [swap(second, ("phys", "cell")), first, sens, got],
    )
    (halves,) = kernel_call(
        functools.partial(second_step_kernel, owners, root_stations),
        "second_step",
        [(3 * share, LANES)],
        [swap_rows(terms), own],
    )
    return tuple(
        kernel_call(layout_kernel, "layout", [(1, rows * LANES)] * 3, [lax.all_gather(halves, "phys")], kept=False)
    )


def solution(mesh):
    return jax.shard_map(
        per_device,
        mesh=mesh,
        in_specs=(
            P("phys", "sta", "cell"),
            P("phys", "sta"),
            P("phys", "sta"),
            P("phys"),
            P("cell"),
        ),
        out_specs=(P("cell", "sta"), P("cell", "sta"), P("cell", "sta")),
        check_vma=False,
    )
```

```python
import functools
import math

import jax
import jax.numpy as jnp
from jax import lax
from jax.experimental import pallas as pl
from jax.experimental.pallas import tpu as pltpu
from jax.sharding import PartitionSpec as P

ITERS = 2
LANES = 128
SUB = 8

step_size = 0.5
weight_floor = 0.1
epsilon = 1e-06


def lane_index(rows):
    return lax.broadcasted_iota(jnp.int32, (rows, LANES), 1)


def as_column(row):
    stations = row.shape[1]
    wide = jnp.broadcast_to(row, (stations, stations))
    at = lax.broadcasted_iota(jnp.int32, (stations, stations), 0)
    to = lax.broadcasted_iota(jnp.int32, (stations, stations), 1)
    return jnp.sum(jnp.where(at == to, wide, 0.0), axis=1, keepdims=True)


def in_lanes(columns):
    lane = lane_index(columns[0].shape[0])
    tile = jnp.zeros(lane.shape, jnp.float32)
    for at, column in enumerate(columns):
        tile = jnp.where(lane == at, column, tile)
    return tile


def lanes_of(chunk):
    return pl.ds(chunk * LANES, LANES)


def fold(values):
    row = lax.broadcasted_iota(jnp.int32, (SUB, LANES), 0)
    skewed = [values[-at % SUB] for at in range(SUB)]
    for shift in (1, 2, 4):
        moves = (row & shift) != 0
        skewed = [jnp.where(moves, skewed[(at - shift) % SUB], skewed[at]) for at in range(SUB)]
    terms = [skewed[0]] + [pltpu.roll(skewed[at], SUB - at, 0) for at in range(1, SUB)]
    return ((terms[0] + terms[1]) + (terms[2] + terms[3])) + ((terms[4] + terms[5]) + (terms[6] + terms[7]))


def store_tiles(owners, size, owner_rows, out):
    group = SUB // math.gcd(SUB, size)
    tiles = group * size // SUB

    for step in range(owners // group):
        values = []
        for member in range(group):
            values += owner_rows(step * group + member)
        for tile in range(tiles):
            out[step * tiles + tile] = fold(values[tile * SUB : (tile + 1) * SUB])


def predict_kernel(
    rows, sens_hbm, model_hbm, observed_hbm, weight_hbm, scale, out, sens, send, model, observed, weight, sems
):
    halves, pieces = sens.shape[0] // SUB, sems.shape[0] - 3
    size = sens.shape[1] // pieces
    share = rows // 2
    core = lax.axis_index("phys")
    small = [
        pltpu.make_async_copy(source, target, sems.at[pieces + at])
        for at, (source, target) in enumerate(
            [(model_hbm, model), (observed_hbm, observed), (weight_hbm, weight)]
        )
    ]
    large = []
    for piece in range(pieces):
        lanes = pl.ds(piece * size, size)
        large.append(pltpu.make_async_copy(sens_hbm.at[:, lanes], sens.at[:, lanes], sems.at[piece]))
    small[0].start()
    for copy in large:
        copy.start()
    for copy in small[1:]:
        copy.start()
    small[0].wait()
    owners = size // LANES // rows

    def body(owner, acc):
        acc = list(acc)
        for row in range(rows):
            at = owner * rows + row
            value = model[pl.ds(at, 1), :]
            for half in range(halves):
                slot = (row % 4) * halves + half
                acc[slot] = acc[slot] + sens[half * SUB : (half + 1) * SUB, lanes_of(at)] * value
        for row in range(share):
            source = lanes_of(owner * rows + (1 - core) * share + row)
            send[:, lanes_of(owner * share + row)] = sens[:, source]
        return tuple(acc)

    acc = (jnp.zeros((SUB, LANES), jnp.float32),) * (4 * halves)
    for piece in range(pieces):
        large[piece].wait()
        for owner in range(piece * owners, (piece + 1) * owners):
            acc = body(owner, acc)
    total = [
        (acc[half] + acc[halves + half]) + (acc[2 * halves + half] + acc[3 * halves + half]) for half in range(halves)
    ]
    part = jnp.sum(jnp.concatenate(total, axis=0), axis=1, keepdims=True)
    for copy in small[1:]:
        copy.wait()
    column = as_column(weight[...])
    tile = in_lanes([part, column, as_column(observed[...]), scale[0] * column])
    for peer in range(out.shape[0]):
        out[peer] = tile


def residual_weights(predicted, station):
    weight, observed, scaled = station[:, 1:2], station[:, 2:3], station[:, 3:4]
    residual = weight * (predicted - observed)
    shape = (station.shape[0], LANES)
    return jnp.broadcast_to(weight * weight, shape), jnp.broadcast_to(scaled * residual, shape)


def first_terms_kernel(rows, owners, cell_blocks, root_cells, parts, sens, got, out, wide):
    halves = sens.shape[0] // SUB
    share = rows // 2
    core = lax.axis_index("phys")
    for place, method in enumerate((core, 1 - core)):
        station = parts[method * cell_blocks]
        total = station
        for block in range(1, cell_blocks):
            total = total + parts[method * cell_blocks + block]
        wide[place], wide[2 + place] = residual_weights(total[:, 0:1] / root_cells, station)

    def owner_rows(owner):
        columns, gradients = ([], []), []
        for row in range(share):
            sources = (
                (sens, lanes_of(owner * rows + core * share + row)),
                (got, lanes_of(owner * share + row)),
            )
            gradient = None
            for method, (source, lanes) in enumerate(sources):
                column = None
                for half in range(halves):
                    at = slice(half * SUB, (half + 1) * SUB)
                    block = source[at, lanes]
                    c = block * block * wide[method, at, :]
                    g = block * wide[2 + method, at, :]
                    column = c if column is None else column + c
                    gradient = g if gradient is None else gradient + g
                columns[method].append(column)
            gradients.append(gradient)
        return columns[0] + columns[1] + gradients

    store_tiles(owners, 3 * share, owner_rows, out)


def owner_sum_kernel(rows, owners, received, own, out):
    share = rows // 2
    core = lax.axis_index("phys")
    size = 3 * share
    for row in range(size):
        own[row : row + 1, :] = jnp.sum(received[pl.ds(row, owners, stride=size), :], axis=0, keepdims=True)
    largest = []
    for method in range(2):
        most = jnp.max(own[method * share : (method + 1) * share, :], axis=0, keepdims=True)
        largest.append(jnp.max(most, axis=1, keepdims=True))
    first = jnp.where(core == 0, largest[0], largest[1])
    second = jnp.where(core == 0, largest[1], largest[0])
    tile = jnp.where(lane_index(1) < LANES // 2, first, second)
    for peer in range(out.shape[0]):
        out[peer] = tile


def message_kernel(owners, maxima, own, out):
    size = own.shape[0] + 1
    most = maxima[0]
    for peer in range(1, maxima.shape[0]):
        most = jnp.maximum(most, maxima[peer])
    for row in range(size):
        value = own[row : row + 1, :] if row < size - 1 else most
        out[pl.ds(row, owners, stride=size), :] = jnp.broadcast_to(value, (owners, LANES))


def model_kernel(rows, owners, physics, root_stations, message, start, sens, got, out, own, model, weights):
    halves = sens.shape[0] // SUB
    share = rows // 2
    core = lax.axis_index("phys")
    position = lax.axis_index("sta")
    size = message.shape[0] // owners
    most = jnp.max(message[pl.ds(size - 1, owners, stride=size), :], axis=0, keepdims=True)
    first_lanes = lane_index(1) < LANES // 2
    scales = []
    for method in (core, 1 - core):
        inside = first_lanes == (method == 0)
        largest = jnp.max(jnp.where(inside, most, 0.0), axis=1, keepdims=True)
        scales.append(1.0 / (largest + epsilon))
    for row in range(share):
        relative = None
        for method in range(2):
            column = message[pl.ds(method * share + row, owners, stride=size), :]
            r = jnp.sqrt(column * scales[method])
            relative = r if relative is None else relative + r
        weight = weight_floor + relative / physics
        summed = message[pl.ds(2 * share + row, owners, stride=size), :]
        before = [start[pl.ds(at * share + row, owners, stride=rows), :] for at in range(2)]
        at = pl.ds(row, owners, stride=share)
        model[at, :] = jnp.where(core == 0, before[0], before[1]) - step_size * (summed / (root_stations * weight))
        weights[at, :] = weight

    def body(owner, acc):
        acc = list(acc)
        for row in range(share):
            value = model[pl.ds(owner * share + row, 1), :]
            sources = (
                (sens, lanes_of(owner * rows + core * share + row)),
                (got, lanes_of(owner * share + row)),
            )
            for method, (source, lanes) in enumerate(sources):
                for half in range(halves):
                    slot = ((row % 2) * 2 + method) * halves + half
                    acc[slot] = acc[slot] + source[half * SUB : (half + 1) * SUB, lanes] * value
        return tuple(acc)

    acc = (jnp.zeros((SUB, LANES), jnp.float32),) * (4 * halves)
    for owner in range(owners):
        acc = body(owner, acc)
    columns = []
    for method in range(2):
        total = [acc[method * halves + half] + acc[(2 + method) * halves + half] for half in range(halves)]
        columns.append(jnp.sum(jnp.concatenate(total, axis=0), axis=1, keepdims=True))
    lane = lane_index(columns[0].shape[0])
    tile = jnp.where(lane == core, columns[0], jnp.where(lane == 1 - core, columns[1], 0.0))
    for peer in range(out.shape[0]):
        out[peer] = tile
    own_rows = pl.ds(position * share, share)
    own[0] = weights[own_rows, :]
    own[1] = model[own_rows, :]


def second_terms_kernel(rows, owners, cell_blocks, root_cells, parts, stations, sens, got, out, wide):
    halves = sens.shape[0] // SUB
    share = rows // 2
    core = lax.axis_index("phys")
    total = parts[0]
    for peer in range(1, parts.shape[0]):
        total = total + parts[peer]
    lane = lane_index(total.shape[0])
    for place, method in enumerate((core, 1 - core)):
        predicted = jnp.sum(jnp.where(lane == method, total, 0.0), axis=1, keepdims=True) / root_cells
        _, wide[place] = residual_weights(predicted, stations[method * cell_blocks])

    def owner_rows(owner):
        gradients = []
        for row in range(share):
            sources = (
                (sens, lanes_of(owner * rows + core * share + row)),
                (got, lanes_of(owner * share + row)),
            )
            gradient = None
            for method, (source, lanes) in enumerate(sources):
                for half in range(halves):
                    at = slice(half * SUB, (half + 1) * SUB)
                    g = source[at, lanes] * wide[method, at, :]
                    gradient = g if gradient is None else gradient + g
            gradients.append(gradient)
        return gradients

    store_tiles(owners, share, owner_rows, out)


def second_step_kernel(owners, root_stations, received, own, out):
    share = own.shape[1]
    for row in range(share):
        total = jnp.sum(received[pl.ds(row, owners, stride=share), :], axis=0, keepdims=True)
        weight = own[0, row : row + 1, :]
        gradient = total / (root_stations * weight)
        out[row : row + 1, :] = weight
        out[share + row : share + row + 1, :] = gradient
        out[2 * share + row : 2 * share + row + 1, :] = own[1, row : row + 1, :] - step_size * gradient


def layout_kernel(both, *outs):
    share = both.shape[1] // len(outs)
    for at, out in enumerate(outs):
        for core in range(both.shape[0]):
            for row in range(share):
                to = (core * share + row) * LANES
                source = at * share + row
                out[:, to : to + LANES] = both[core, source : source + 1, :]


def kernel_call(kernel, name, outs, operands, scratch=(), spaces=None, kept=True):
    make = pltpu.VMEM if kept else jax.ShapeDtypeStruct
    spaces = spaces or [pltpu.VMEM] * len(operands)
    operands = [
        pltpu.with_memory_space_constraint(x, space) if space == pltpu.HBM else x for x, space in zip(operands, spaces)
    ]
    return pl.pallas_call(
        kernel,
        name=name,
        out_shape=[make(shape, jnp.float32) for shape in outs],
        in_specs=[pl.BlockSpec(memory_space=space) for space in spaces],
        out_specs=[pl.BlockSpec(memory_space=pltpu.VMEM)] * len(outs),
        scratch_shapes=scratch,
        compiler_params=pltpu.CompilerParams(vmem_limit_bytes=16 * 2**20),
    )(*operands)


def per_device(sensitivity, observed, data_weight, phys_weight, start_model):
    owners = lax.axis_size("sta")
    cell_blocks = lax.axis_size("cell")
    physics = sensitivity.shape[0] * lax.axis_size("phys")
    stations, cell_count = sensitivity.shape[1:]
    chunks = cell_count // LANES
    rows = chunks // owners
    share = rows // 2
    root_cells = math.sqrt(cell_count * cell_blocks)
    root_stations = math.sqrt(stations * owners)
    sens = sensitivity.reshape(stations, cell_count)
    start = start_model.reshape(chunks, LANES)
    peers = physics * cell_blocks
    pieces = min(8, owners)

    def swap(array, axes):
        return lax.all_to_all(array, axes, 0, 0, tiled=True)

    def swap_rows(array):
        return swap(array.reshape(owners, 1, -1), "sta").reshape(-1, LANES)

    parts_shape = (peers, stations, LANES)
    first, sens, send = kernel_call(
        functools.partial(predict_kernel, rows),
        "predict",
        [parts_shape, (stations, cell_count), (stations, cell_count // 2)],
        [sens, start, observed, data_weight, phys_weight],
        scratch=[
            pltpu.VMEM((chunks, LANES), jnp.float32),
            pltpu.VMEM((1, stations), jnp.float32),
            pltpu.VMEM((1, stations), jnp.float32),
            pltpu.SemaphoreType.DMA((pieces + 3,)),
        ],
        spaces=[pltpu.HBM] * 4 + [pltpu.SMEM],
    )
    got = lax.ppermute(send, "phys", [(0, 1), (1, 0)])
    first = swap(first, ("phys", "cell"))
    (terms,) = kernel_call(
        functools.partial(first_terms_kernel, rows, owners, cell_blocks, root_cells),
        "first_terms",
        [(owners * 3 * share // SUB, SUB, LANES)],
        [first, sens, got],
        scratch=[pltpu.VMEM((4, stations, LANES), jnp.float32)],
    )
    own, maxima = kernel_call(
        functools.partial(owner_sum_kernel, rows, owners),
        "owner_sum",
        [(3 * share, LANES), (peers, 1, LANES)],
        [swap_rows(terms)],
    )
    (message,) = kernel_call(
        functools.partial(message_kernel, owners),
        "message",
        [(owners * (3 * share + 1), LANES)],
        [swap(maxima, ("phys", "cell")), own],
    )
    second, own = kernel_call(
        functools.partial(model_kernel, rows, owners, physics, root_stations),
        "model",
        [parts_shape, (2, share, LANES)],
        [swap_rows(message), start, sens, got],
        scratch=[pltpu.VMEM((chunks // 2, LANES), jnp.float32)] * 2,
    )
    (terms,) = kernel_call(
        functools.partial(second_terms_kernel, rows, owners, cell_blocks, root_cells),
        "second_terms",
        [(owners * share // SUB, SUB, LANES)],
        [swap(second, ("phys", "cell")), first, sens, got],
        scratch=[pltpu.VMEM((2, stations, LANES), jnp.float32)],
    )
    (halves,) = kernel_call(
        functools.partial(second_step_kernel, owners, root_stations),
        "second_step",
        [(3 * share, LANES)],
        [swap_rows(terms), own],
    )
    return tuple(
        kernel_call(layout_kernel, "layout", [(1, rows * LANES)] * 3, [lax.all_gather(halves, "phys")], kept=False)
    )


def solution(mesh):
    return jax.shard_map(
        per_device,
        mesh=mesh,
        in_specs=(
            P("phys", "sta", "cell"),
            P("phys", "sta"),
            P("phys", "sta"),
            P("phys"),
            P("cell"),
        ),
        out_specs=(P("cell", "sta"), P("cell", "sta"), P("cell", "sta")),
        check_vma=False,
    )
```

```python
import functools
import math

import jax
import jax.numpy as jnp
from jax import lax
from jax.experimental import pallas as pl
from jax.experimental.pallas import tpu as pltpu
from jax.sharding import PartitionSpec as P

ITERS = 2
LANES = 128
SUB = 8

step_size = 0.5
weight_floor = 0.1
epsilon = 1e-06


def lane_index(rows):
    return lax.broadcasted_iota(jnp.int32, (rows, LANES), 1)


def as_column(row):
    stations = row.shape[1]
    wide = jnp.broadcast_to(row, (stations, stations))
    at = lax.broadcasted_iota(jnp.int32, (stations, stations), 0)
    to = lax.broadcasted_iota(jnp.int32, (stations, stations), 1)
    return jnp.sum(jnp.where(at == to, wide, 0.0), axis=1, keepdims=True)


def in_lanes(columns):
    lane = lane_index(columns[0].shape[0])
    tile = jnp.zeros(lane.shape, jnp.float32)
    for at, column in enumerate(columns):
        tile = jnp.where(lane == at, column, tile)
    return tile


def lanes_of(chunk):
    return pl.ds(chunk * LANES, LANES)


def fold(values):
    row = lax.broadcasted_iota(jnp.int32, (SUB, LANES), 0)
    skewed = [values[-at % SUB] for at in range(SUB)]
    for shift in (1, 2, 4):
        moves = (row & shift) != 0
        skewed = [jnp.where(moves, skewed[(at - shift) % SUB], skewed[at]) for at in range(SUB)]
    terms = [skewed[0]] + [pltpu.roll(skewed[at], SUB - at, 0) for at in range(1, SUB)]
    return ((terms[0] + terms[1]) + (terms[2] + terms[3])) + ((terms[4] + terms[5]) + (terms[6] + terms[7]))


def store_tiles(owners, size, owner_rows, out):
    group = SUB // math.gcd(SUB, size)
    tiles = group * size // SUB

    for step in range(owners // group):
        values = []
        for member in range(group):
            values += owner_rows(step * group + member)
        for tile in range(tiles):
            out[step * tiles + tile] = fold(values[tile * SUB : (tile + 1) * SUB])


def predict_kernel(
    rows, sens_hbm, model_hbm, observed_hbm, weight_hbm, scale, out, sens, model, observed, weight, sems
):
    halves, pieces = sens.shape[0] // SUB, sems.shape[0] - 3
    size = sens.shape[1] // pieces
    small = [
        pltpu.make_async_copy(source, target, sems.at[pieces + at])
        for at, (source, target) in enumerate(
            [(model_hbm, model), (observed_hbm, observed), (weight_hbm, weight)]
        )
    ]
    large = []
    for piece in range(pieces):
        lanes = pl.ds(piece * size, size)
        large.append(pltpu.make_async_copy(sens_hbm.at[:, lanes], sens.at[:, lanes], sems.at[piece]))
    small[0].start()
    for copy in large:
        copy.start()
    for copy in small[1:]:
        copy.start()
    small[0].wait()
    owners = size // LANES // rows

    def body(owner, acc):
        acc = list(acc)
        for row in range(rows):
            at = owner * rows + row
            value = model[pl.ds(at, 1), :]
            for half in range(halves):
                slot = (row % 4) * halves + half
                acc[slot] = acc[slot] + sens[half * SUB : (half + 1) * SUB, lanes_of(at)] * value
        return tuple(acc)

    acc = (jnp.zeros((SUB, LANES), jnp.float32),) * (4 * halves)
    for piece in range(pieces):
        large[piece].wait()
        for owner in range(piece * owners, (piece + 1) * owners):
            acc = body(owner, acc)
    total = [
        (acc[half] + acc[halves + half]) + (acc[2 * halves + half] + acc[3 * halves + half]) for half in range(halves)
    ]
    part = jnp.sum(jnp.concatenate(total, axis=0), axis=1, keepdims=True)
    for copy in small[1:]:
        copy.wait()
    column = as_column(weight[...])
    tile = in_lanes([part, column, as_column(observed[...]), scale[0] * column])
    for peer in range(out.shape[0]):
        out[peer] = tile


def residual_weights(predicted, station):
    weight, observed, scaled = station[:, 1:2], station[:, 2:3], station[:, 3:4]
    residual = weight * (predicted - observed)
    shape = (station.shape[0], LANES)
    return jnp.broadcast_to(weight * weight, shape), jnp.broadcast_to(scaled * residual, shape)


def first_terms_kernel(rows, owners, cell_blocks, root_cells, parts, sens, got, out, wide):
    halves = sens.shape[0] // SUB
    share = rows // 2
    core = lax.axis_index("phys")
    for place, method in enumerate((core, 1 - core)):
        station = parts[method * cell_blocks]
        total = station
        for block in range(1, cell_blocks):
            total = total + parts[method * cell_blocks + block]
        wide[place], wide[2 + place] = residual_weights(total[:, 0:1] / root_cells, station)

    def owner_rows(owner):
        columns, gradients = ([], []), []
        for row in range(share):
            lanes = lanes_of(owner * rows + core * share + row)
            gradient = None
            for method, source in enumerate((sens, got)):
                column = None
                for half in range(halves):
                    at = slice(half * SUB, (half + 1) * SUB)
                    block = source[at, lanes]
                    c = block * block * wide[method, at, :]
                    g = block * wide[2 + method, at, :]
                    column = c if column is None else column + c
                    gradient = g if gradient is None else gradient + g
                columns[method].append(column)
            gradients.append(gradient)
        return columns[0] + columns[1] + gradients

    store_tiles(owners, 3 * share, owner_rows, out)


def owner_sum_kernel(rows, owners, received, out):
    share = rows // 2
    core = lax.axis_index("phys")
    size = 3 * share
    sums = [jnp.sum(received[pl.ds(row, owners, stride=size), :], axis=0, keepdims=True) for row in range(size)]
    mine, other, gradient = sums[:share], sums[share : 2 * share], sums[2 * share :]
    columns = [jnp.where(core == 0, a, b) for a, b in zip(mine + other, other + mine)]
    largest = []
    for method in range(2):
        most = functools.reduce(jnp.maximum, columns[method * share : (method + 1) * share])
        largest.append(jnp.max(most, axis=1, keepdims=True))
    most = jnp.where(lane_index(1) < LANES // 2, largest[0], largest[1])
    fill = [jnp.zeros((out.shape[1] - size - 1, LANES), jnp.float32)] if out.shape[1] > size + 1 else []
    tile = jnp.concatenate(columns + gradient + [most] + fill, axis=0)
    for peer in range(out.shape[0]):
        out[peer] = tile


def message_kernel(rows, owners, cell_blocks, slices, out):
    size = 3 * (rows // 2) + 1
    core = lax.axis_index("phys")
    own = slices[core * cell_blocks + lax.axis_index("cell")]
    most = slices[0, size - 1 : size, :]
    for peer in range(1, slices.shape[0]):
        most = jnp.maximum(most, slices[peer, size - 1 : size, :])
    for row in range(size):
        value = own[row : row + 1] if row < size - 1 else most
        out[pl.ds(row, owners, stride=size), :] = jnp.broadcast_to(value, (owners, LANES))


def model_kernel(
    rows, owners, cell_blocks, physics, root_stations, message, slices, start, sens, got, out, own, model
):
    halves = sens.shape[0] // SUB
    share = rows // 2
    core = lax.axis_index("phys")
    position = lax.axis_index("sta")
    size = message.shape[0] // owners
    most = jnp.max(message[pl.ds(size - 1, owners, stride=size), :], axis=0, keepdims=True)
    first_lanes = lane_index(1) < LANES // 2
    scales = []
    for inside in (first_lanes, ~first_lanes):
        largest = jnp.max(jnp.where(inside, most, 0.0), axis=1, keepdims=True)
        scales.append(1.0 / (largest + epsilon))

    def step(before, columns, summed):
        relative = None
        for column, scale in zip(columns, scales):
            r = jnp.sqrt(column * scale)
            relative = r if relative is None else relative + r
        weight = weight_floor + relative / physics
        return weight, before - step_size * (summed / (root_stations * weight))

    for row in range(share):
        columns = [message[pl.ds(method * share + row, owners, stride=size), :] for method in range(2)]
        summed = message[pl.ds(2 * share + row, owners, stride=size), :]
        before = [start[pl.ds(at * share + row, owners, stride=rows), :] for at in range(2)]
        before = jnp.where(core == 0, before[0], before[1])
        model[pl.ds(row, owners, stride=share), :] = step(before, columns, summed)[1]

    before = start[pl.ds(position * rows, rows), :]
    for half in range(2):
        place = half * cell_blocks + lax.axis_index("cell")
        columns = [slices[place, method * share : (method + 1) * share, :] for method in range(2)]
        summed = slices[place, 2 * share : 3 * share, :]
        at = slice(half * share, (half + 1) * share)
        own[0, at, :], own[1, at, :] = step(before[at], columns, summed)

    def body(owner, acc):
        acc = list(acc)
        for row in range(share):
            value = model[pl.ds(owner * share + row, 1), :]
            lanes = lanes_of(owner * rows + core * share + row)
            for method, source in enumerate((sens, got)):
                for half in range(halves):
                    slot = ((row % 2) * 2 + method) * halves + half
                    acc[slot] = acc[slot] + source[half * SUB : (half + 1) * SUB, lanes] * value
        return tuple(acc)

    acc = (jnp.zeros((SUB, LANES), jnp.float32),) * (4 * halves)
    for owner in range(owners):
        acc = body(owner, acc)
    columns = []
    for method in range(2):
        total = [acc[method * halves + half] + acc[(2 + method) * halves + half] for half in range(halves)]
        columns.append(jnp.sum(jnp.concatenate(total, axis=0), axis=1, keepdims=True))
    lane = lane_index(columns[0].shape[0])
    tile = jnp.where(lane == core, columns[0], jnp.where(lane == 1 - core, columns[1], 0.0))
    for peer in range(out.shape[0]):
        out[peer] = tile


def second_terms_kernel(rows, owners, cell_blocks, root_cells, parts, stations, sens, got, out, wide):
    halves = sens.shape[0] // SUB
    core = lax.axis_index("phys")
    total = parts[0]
    for peer in range(1, parts.shape[0]):
        total = total + parts[peer]
    lane = lane_index(total.shape[0])
    for place, method in enumerate((core, 1 - core)):
        predicted = jnp.sum(jnp.where(lane == method, total, 0.0), axis=1, keepdims=True) / root_cells
        _, wide[place] = residual_weights(predicted, stations[method * cell_blocks])

    def owner_rows(owner):
        gradients = []
        for row in range(rows):
            lanes = lanes_of(owner * rows + row)
            gradient = None
            for method, source in enumerate((sens, got)):
                for half in range(halves):
                    at = slice(half * SUB, (half + 1) * SUB)
                    g = source[at, lanes] * wide[method, at, :]
                    gradient = g if gradient is None else gradient + g
            gradients.append(gradient)
        return gradients

    store_tiles(owners, rows, owner_rows, out)


def second_step_kernel(owners, root_stations, received, own, weight_out, gradient_out, model_out):
    rows = own.shape[1]
    for row in range(rows):
        total = jnp.sum(received[pl.ds(row, owners, stride=rows), :], axis=0, keepdims=True)
        weight = own[0, row : row + 1, :]
        gradient = total / (root_stations * weight)
        lanes = slice(row * LANES, (row + 1) * LANES)
        weight_out[:, lanes] = weight
        gradient_out[:, lanes] = gradient
        model_out[:, lanes] = own[1, row : row + 1, :] - step_size * gradient


def kernel_call(kernel, name, outs, operands, scratch=(), spaces=None, kept=True):
    make = pltpu.VMEM if kept else jax.ShapeDtypeStruct
    spaces = spaces or [pltpu.VMEM] * len(operands)
    operands = [
        pltpu.with_memory_space_constraint(x, space) if space == pltpu.HBM else x for x, space in zip(operands, spaces)
    ]
    return pl.pallas_call(
        kernel,
        name=name,
        out_shape=[make(shape, jnp.float32) for shape in outs],
        in_specs=[pl.BlockSpec(memory_space=space) for space in spaces],
        out_specs=[pl.BlockSpec(memory_space=pltpu.VMEM)] * len(outs),
        scratch_shapes=scratch,
        compiler_params=pltpu.CompilerParams(vmem_limit_bytes=16 * 2**20),
    )(*operands)


def per_device(sensitivity, observed, data_weight, phys_weight, start_model):
    owners = lax.axis_size("sta")
    cell_blocks = lax.axis_size("cell")
    physics = sensitivity.shape[0] * lax.axis_size("phys")
    stations, cell_count = sensitivity.shape[1:]
    chunks = cell_count // LANES
    rows = chunks // owners
    share = rows // 2
    root_cells = math.sqrt(cell_count * cell_blocks)
    root_stations = math.sqrt(stations * owners)
    sens = sensitivity.reshape(stations, cell_count)
    start = start_model.reshape(chunks, LANES)
    peers = physics * cell_blocks
    pieces = min(8, owners)

    def swap(array, axes):
        return lax.all_to_all(array, axes, 0, 0, tiled=True)

    def swap_rows(array):
        return swap(array.reshape(owners, 1, -1), "sta").reshape(-1, LANES)

    parts_shape = (peers, stations, LANES)
    first, sens = kernel_call(
        functools.partial(predict_kernel, rows),
        "predict",
        [parts_shape, (stations, cell_count)],
        [sens, start, observed, data_weight, phys_weight],
        scratch=[
            pltpu.VMEM((chunks, LANES), jnp.float32),
            pltpu.VMEM((1, stations), jnp.float32),
            pltpu.VMEM((1, stations), jnp.float32),
            pltpu.SemaphoreType.DMA((pieces + 3,)),
        ],
        spaces=[pltpu.HBM] * 4 + [pltpu.SMEM],
    )
    got = lax.ppermute(sens, "phys", [(0, 1), (1, 0)])
    first = swap(first, ("phys", "cell"))
    (terms,) = kernel_call(
        functools.partial(first_terms_kernel, rows, owners, cell_blocks, root_cells),
        "first_terms",
        [(owners * 3 * share // SUB, SUB, LANES)],
        [first, sens, got],
        scratch=[pltpu.VMEM((4, stations, LANES), jnp.float32)],
    )
    size = 3 * share + 1
    (slices,) = kernel_call(
        functools.partial(owner_sum_kernel, rows, owners),
        "owner_sum",
        [(peers, -(-size // SUB) * SUB, LANES)],
        [swap_rows(terms)],
    )
    slices = swap(slices, ("phys", "cell"))
    (message,) = kernel_call(
        functools.partial(message_kernel, rows, owners, cell_blocks),
        "message",
        [(owners * size, LANES)],
        [slices],
    )
    second, own = kernel_call(
        functools.partial(model_kernel, rows, owners, cell_blocks, physics, root_stations),
        "model",
        [parts_shape, (2, rows, LANES)],
        [swap_rows(message), slices, start, sens, got],
        scratch=[pltpu.VMEM((chunks // 2, LANES), jnp.float32)],
    )
    (terms,) = kernel_call(
        functools.partial(second_terms_kernel, rows, owners, cell_blocks, root_cells),
        "second_terms",
        [(chunks // SUB, SUB, LANES)],
        [swap(second, ("phys", "cell")), first, sens, got],
        scratch=[pltpu.VMEM((2, stations, LANES), jnp.float32)],
    )
    return tuple(
        kernel_call(
            functools.partial(second_step_kernel, owners, root_stations),
            "second_step",
            [(1, rows * LANES)] * 3,
            [swap_rows(terms), own],
            kept=False,
        )
    )


def solution(mesh):
    return jax.shard_map(
        per_device,
        mesh=mesh,
        in_specs=(
            P("phys", "sta", "cell"),
            P("phys", "sta"),
            P("phys", "sta"),
            P("phys"),
            P("cell"),
        ),
        out_specs=(P("cell", "sta"), P("cell", "sta"), P("cell", "sta")),
        check_vma=False,
    )
```

```python
import functools
import math

import jax
import jax.numpy as jnp
from jax import lax
from jax.experimental import pallas as pl
from jax.experimental.pallas import tpu as pltpu
from jax.sharding import PartitionSpec as P

ITERS = 2
LANES = 128
SUB = 8

step_size = 0.5
weight_floor = 0.1
epsilon = 1e-06

RANK_BITS = (0, 2, 3, 5, 4, 1)


def bit_names(owners):
    return tuple(f"sta_{bit}" for bit in range(owners.bit_length() - 1))


def rank_bits(owners):
    bits = range(len(bit_names(owners)))
    return RANK_BITS if len(RANK_BITS) == len(bits) else tuple(bits)


def owner_of_rank(owners):
    bits = rank_bits(owners)
    last = len(bits) - 1
    return [sum((rank >> (last - at) & 1) << (last - bit) for at, bit in enumerate(bits)) for rank in range(owners)]


def sta_index(owners):
    index = 0
    for name in bit_names(owners):
        index = index * 2 + lax.axis_index(name)
    return index


def lane_index(rows):
    return lax.broadcasted_iota(jnp.int32, (rows, LANES), 1)


def as_column(row):
    stations = row.shape[1]
    wide = jnp.broadcast_to(row, (stations, stations))
    at = lax.broadcasted_iota(jnp.int32, (stations, stations), 0)
    to = lax.broadcasted_iota(jnp.int32, (stations, stations), 1)
    return jnp.sum(jnp.where(at == to, wide, 0.0), axis=1, keepdims=True)


def in_lanes(columns):
    lane = lane_index(columns[0].shape[0])
    tile = jnp.zeros(lane.shape, jnp.float32)
    for at, column in enumerate(columns):
        tile = jnp.where(lane == at, column, tile)
    return tile


def lanes_of(chunk):
    return pl.ds(chunk * LANES, LANES)


def fold(values):
    row = lax.broadcasted_iota(jnp.int32, (SUB, LANES), 0)
    skewed = [values[-at % SUB] for at in range(SUB)]
    for shift in (1, 2, 4):
        moves = (row & shift) != 0
        skewed = [jnp.where(moves, skewed[(at - shift) % SUB], skewed[at]) for at in range(SUB)]
    terms = [skewed[0]] + [pltpu.roll(skewed[at], SUB - at, 0) for at in range(1, SUB)]
    return ((terms[0] + terms[1]) + (terms[2] + terms[3])) + ((terms[4] + terms[5]) + (terms[6] + terms[7]))


def store_tiles(owners, size, owner_rows, out):
    places = owner_of_rank(owners)
    group = SUB // math.gcd(SUB, size)
    tiles = group * size // SUB

    for step in range(owners // group):
        values = []
        for member in range(group):
            values += owner_rows(places[step * group + member])
        for tile in range(tiles):
            out[step * tiles + tile] = fold(values[tile * SUB : (tile + 1) * SUB])


def predict_kernel(
    rows, sens_hbm, model_hbm, observed_hbm, weight_hbm, scale, out, sens, model, observed, weight, sems
):
    halves, pieces = sens.shape[0] // SUB, sems.shape[0] - 3
    size = sens.shape[1] // pieces
    small = [
        pltpu.make_async_copy(source, target, sems.at[pieces + at])
        for at, (source, target) in enumerate(
            [(model_hbm, model), (observed_hbm, observed), (weight_hbm, weight)]
        )
    ]
    large = []
    for piece in range(pieces):
        lanes = pl.ds(piece * size, size)
        large.append(pltpu.make_async_copy(sens_hbm.at[:, lanes], sens.at[:, lanes], sems.at[piece]))
    small[0].start()
    for copy in large:
        copy.start()
    for copy in small[1:]:
        copy.start()
    small[0].wait()
    owners = size // LANES // rows

    def body(owner, acc):
        acc = list(acc)
        for row in range(rows):
            at = owner * rows + row
            value = model[pl.ds(at, 1), :]
            for half in range(halves):
                slot = (row % 4) * halves + half
                acc[slot] = acc[slot] + sens[half * SUB : (half + 1) * SUB, lanes_of(at)] * value
        return tuple(acc)

    acc = (jnp.zeros((SUB, LANES), jnp.float32),) * (4 * halves)
    for piece in range(pieces):
        large[piece].wait()
        for owner in range(piece * owners, (piece + 1) * owners):
            acc = body(owner, acc)
    total = [
        (acc[half] + acc[halves + half]) + (acc[2 * halves + half] + acc[3 * halves + half]) for half in range(halves)
    ]
    part = jnp.sum(jnp.concatenate(total, axis=0), axis=1, keepdims=True)
    for copy in small[1:]:
        copy.wait()
    column = as_column(weight[...])
    tile = in_lanes([part, column, as_column(observed[...]), scale[0] * column])
    for peer in range(out.shape[0]):
        out[peer] = tile


def residual_weights(predicted, station):
    weight, observed, scaled = station[:, 1:2], station[:, 2:3], station[:, 3:4]
    residual = weight * (predicted - observed)
    shape = (station.shape[0], LANES)
    return jnp.broadcast_to(weight * weight, shape), jnp.broadcast_to(scaled * residual, shape)


def first_terms_kernel(rows, owners, cell_blocks, root_cells, parts, sens, got, out, wide):
    halves = sens.shape[0] // SUB
    share = rows // 2
    core = lax.axis_index("phys")
    for place, method in enumerate((core, 1 - core)):
        station = parts[method * cell_blocks]
        total = station
        for block in range(1, cell_blocks):
            total = total + parts[method * cell_blocks + block]
        wide[place], wide[2 + place] = residual_weights(total[:, 0:1] / root_cells, station)

    def owner_rows(owner):
        columns, gradients = ([], []), []
        for row in range(share):
            lanes = lanes_of(owner * rows + core * share + row)
            gradient = None
            for method, source in enumerate((sens, got)):
                column = None
                for half in range(halves):
                    at = slice(half * SUB, (half + 1) * SUB)
                    block = source[at, lanes]
                    c = block * block * wide[method, at, :]
                    g = block * wide[2 + method, at, :]
                    column = c if column is None else column + c
                    gradient = g if gradient is None else gradient + g
                columns[method].append(column)
            gradients.append(gradient)
        return columns[0] + columns[1] + gradients

    store_tiles(owners, 3 * share, owner_rows, out)


def owner_sum_kernel(rows, owners, received, out):
    share = rows // 2
    core = lax.axis_index("phys")
    size = 3 * share
    sums = [jnp.sum(received[pl.ds(row, owners, stride=size), :], axis=0, keepdims=True) for row in range(size)]
    mine, other, gradient = sums[:share], sums[share : 2 * share], sums[2 * share :]
    columns = [jnp.where(core == 0, a, b) for a, b in zip(mine + other, other + mine)]
    largest = []
    for method in range(2):
        most = functools.reduce(jnp.maximum, columns[method * share : (method + 1) * share])
        largest.append(jnp.max(most, axis=1, keepdims=True))
    most = jnp.where(lane_index(1) < LANES // 2, largest[0], largest[1])
    fill = [jnp.zeros((out.shape[1] - size - 1, LANES), jnp.float32)] if out.shape[1] > size + 1 else []
    tile = jnp.concatenate(columns + gradient + [most] + fill, axis=0)
    for peer in range(out.shape[0]):
        out[peer] = tile


def message_kernel(rows, owners, cell_blocks, slices, out):
    size = 3 * (rows // 2) + 1
    core = lax.axis_index("phys")
    own = slices[core * cell_blocks + lax.axis_index("cell")]
    most = slices[0, size - 1 : size, :]
    for peer in range(1, slices.shape[0]):
        most = jnp.maximum(most, slices[peer, size - 1 : size, :])
    for row in range(size):
        value = own[row : row + 1] if row < size - 1 else most
        out[pl.ds(row, owners, stride=size), :] = jnp.broadcast_to(value, (owners, LANES))


def model_kernel(
    rows, owners, cell_blocks, physics, root_stations, message, slices, start, sens, got, out, own, model
):
    halves = sens.shape[0] // SUB
    share = rows // 2
    core = lax.axis_index("phys")
    position = sta_index(owners)
    places = owner_of_rank(owners)
    size = message.shape[0] // owners
    most = jnp.max(message[pl.ds(size - 1, owners, stride=size), :], axis=0, keepdims=True)
    first_lanes = lane_index(1) < LANES // 2
    scales = []
    for inside in (first_lanes, ~first_lanes):
        largest = jnp.max(jnp.where(inside, most, 0.0), axis=1, keepdims=True)
        scales.append(1.0 / (largest + epsilon))

    def step(before, columns, summed):
        relative = None
        for column, scale in zip(columns, scales):
            r = jnp.sqrt(column * scale)
            relative = r if relative is None else relative + r
        weight = weight_floor + relative / physics
        return weight, before - step_size * (summed / (root_stations * weight))

    for rank, owner in enumerate(places):
        before = [start[owner * rows + half * share : owner * rows + (half + 1) * share, :] for half in range(2)]
        model[rank * share : (rank + 1) * share, :] = jnp.where(core == 0, before[0], before[1])
    for row in range(share):
        columns = [message[pl.ds(method * share + row, owners, stride=size), :] for method in range(2)]
        summed = message[pl.ds(2 * share + row, owners, stride=size), :]
        at = pl.ds(row, owners, stride=share)
        model[at, :] = step(model[at, :], columns, summed)[1]

    before = start[pl.ds(position * rows, rows), :]
    for half in range(2):
        place = half * cell_blocks + lax.axis_index("cell")
        columns = [slices[place, method * share : (method + 1) * share, :] for method in range(2)]
        summed = slices[place, 2 * share : 3 * share, :]
        at = slice(half * share, (half + 1) * share)
        own[0, at, :], own[1, at, :] = step(before[at], columns, summed)

    def body(rank, acc):
        acc = list(acc)
        for row in range(share):
            value = model[pl.ds(rank * share + row, 1), :]
            lanes = lanes_of(places[rank] * rows + core * share + row)
            for method, source in enumerate((sens, got)):
                for half in range(halves):
                    slot = ((row % 2) * 2 + method) * halves + half
                    acc[slot] = acc[slot] + source[half * SUB : (half + 1) * SUB, lanes] * value
        return tuple(acc)

    acc = (jnp.zeros((SUB, LANES), jnp.float32),) * (4 * halves)
    for rank in range(owners):
        acc = body(rank, acc)
    columns = []
    for method in range(2):
        total = [acc[method * halves + half] + acc[(2 + method) * halves + half] for half in range(halves)]
        columns.append(jnp.sum(jnp.concatenate(total, axis=0), axis=1, keepdims=True))
    lane = lane_index(columns[0].shape[0])
    tile = jnp.where(lane == core, columns[0], jnp.where(lane == 1 - core, columns[1], 0.0))
    for peer in range(out.shape[0]):
        out[peer] = tile


def second_terms_kernel(rows, owners, cell_blocks, root_cells, parts, stations, sens, got, out, wide):
    halves = sens.shape[0] // SUB
    core = lax.axis_index("phys")
    total = parts[0]
    for peer in range(1, parts.shape[0]):
        total = total + parts[peer]
    lane = lane_index(total.shape[0])
    for place, method in enumerate((core, 1 - core)):
        predicted = jnp.sum(jnp.where(lane == method, total, 0.0), axis=1, keepdims=True) / root_cells
        _, wide[place] = residual_weights(predicted, stations[method * cell_blocks])

    def owner_rows(owner):
        gradients = []
        for row in range(rows):
            lanes = lanes_of(owner * rows + row)
            gradient = None
            for method, source in enumerate((sens, got)):
                for half in range(halves):
                    at = slice(half * SUB, (half + 1) * SUB)
                    g = source[at, lanes] * wide[method, at, :]
                    gradient = g if gradient is None else gradient + g
            gradients.append(gradient)
        return gradients

    store_tiles(owners, rows, owner_rows, out)


def second_step_kernel(owners, root_stations, received, own, weight_out, gradient_out, model_out):
    rows = own.shape[1]
    for row in range(rows):
        total = jnp.sum(received[pl.ds(row, owners, stride=rows), :], axis=0, keepdims=True)
        weight = own[0, row : row + 1, :]
        gradient = total / (root_stations * weight)
        lanes = slice(row * LANES, (row + 1) * LANES)
        weight_out[:, lanes] = weight
        gradient_out[:, lanes] = gradient
        model_out[:, lanes] = own[1, row : row + 1, :] - step_size * gradient


def kernel_call(kernel, name, outs, operands, scratch=(), spaces=None, kept=True):
    make = pltpu.VMEM if kept else jax.ShapeDtypeStruct
    spaces = spaces or [pltpu.VMEM] * len(operands)
    operands = [
        pltpu.with_memory_space_constraint(x, space) if space == pltpu.HBM else x for x, space in zip(operands, spaces)
    ]
    return pl.pallas_call(
        kernel,
        name=name,
        out_shape=[make(shape, jnp.float32) for shape in outs],
        in_specs=[pl.BlockSpec(memory_space=space) for space in spaces],
        out_specs=[pl.BlockSpec(memory_space=pltpu.VMEM)] * len(outs),
        scratch_shapes=scratch,
        compiler_params=pltpu.CompilerParams(vmem_limit_bytes=16 * 2**20),
    )(*operands)


def per_device(sta, sensitivity, observed, data_weight, phys_weight, start_model):
    owners = math.prod(lax.axis_size(name) for name in sta)
    cell_blocks = lax.axis_size("cell")
    physics = sensitivity.shape[0] * lax.axis_size("phys")
    stations, cell_count = sensitivity.shape[1:]
    chunks = cell_count // LANES
    rows = chunks // owners
    share = rows // 2
    root_cells = math.sqrt(cell_count * cell_blocks)
    root_stations = math.sqrt(stations * owners)
    sens = sensitivity.reshape(stations, cell_count)
    start = start_model.reshape(chunks, LANES)
    peers = physics * cell_blocks
    pieces = min(8, owners)

    def swap(array, axes):
        return lax.all_to_all(array, axes, 0, 0, tiled=True)

    def swap_rows(array):
        return swap(array.reshape(owners, 1, -1), tuple(sta[bit] for bit in rank_bits(owners))).reshape(-1, LANES)

    parts_shape = (peers, stations, LANES)
    first, sens = kernel_call(
        functools.partial(predict_kernel, rows),
        "predict",
        [parts_shape, (stations, cell_count)],
        [sens, start, observed, data_weight, phys_weight],
        scratch=[
            pltpu.VMEM((chunks, LANES), jnp.float32),
            pltpu.VMEM((1, stations), jnp.float32),
            pltpu.VMEM((1, stations), jnp.float32),
            pltpu.SemaphoreType.DMA((pieces + 3,)),
        ],
        spaces=[pltpu.HBM] * 4 + [pltpu.SMEM],
    )
    got = lax.ppermute(sens, "phys", [(0, 1), (1, 0)])
    first = swap(first, ("phys", "cell"))
    (terms,) = kernel_call(
        functools.partial(first_terms_kernel, rows, owners, cell_blocks, root_cells),
        "first_terms",
        [(owners * 3 * share // SUB, SUB, LANES)],
        [first, sens, got],
        scratch=[pltpu.VMEM((4, stations, LANES), jnp.float32)],
    )
    size = 3 * share + 1
    (slices,) = kernel_call(
        functools.partial(owner_sum_kernel, rows, owners),
        "owner_sum",
        [(peers, -(-size // SUB) * SUB, LANES)],
        [swap_rows(terms)],
    )
    slices = swap(slices, ("phys", "cell"))
    (message,) = kernel_call(
        functools.partial(message_kernel, rows, owners, cell_blocks),
        "message",
        [(owners * size, LANES)],
        [slices],
    )
    second, own = kernel_call(
        functools.partial(model_kernel, rows, owners, cell_blocks, physics, root_stations),
        "model",
        [parts_shape, (2, rows, LANES)],
        [swap_rows(message), slices, start, sens, got],
        scratch=[pltpu.VMEM((chunks // 2, LANES), jnp.float32)],
    )
    (terms,) = kernel_call(
        functools.partial(second_terms_kernel, rows, owners, cell_blocks, root_cells),
        "second_terms",
        [(chunks // SUB, SUB, LANES)],
        [swap(second, ("phys", "cell")), first, sens, got],
        scratch=[pltpu.VMEM((2, stations, LANES), jnp.float32)],
    )
    return tuple(
        kernel_call(
            functools.partial(second_step_kernel, owners, root_stations),
            "second_step",
            [(1, rows * LANES)] * 3,
            [swap_rows(terms), own],
            kept=False,
        )
    )


def solution(mesh):
    owners = mesh.shape["sta"]
    sta = bit_names(owners)
    split = jax.sharding.Mesh(
        mesh.devices.reshape((mesh.shape["phys"],) + (2,) * len(sta) + (mesh.shape["cell"],)), ("phys",) + sta + ("cell",)
    )
    return jax.shard_map(
        functools.partial(per_device, sta),
        mesh=split,
        in_specs=(
            P("phys", sta, "cell"),
            P("phys", sta),
            P("phys", sta),
            P("phys"),
            P("cell"),
        ),
        out_specs=(P("cell", sta),) * 3,
        check_vma=False,
    )
```

```python
import functools
import math

import jax
import jax.numpy as jnp
from jax import lax
from jax.experimental import pallas as pl
from jax.experimental.pallas import tpu as pltpu
from jax.sharding import PartitionSpec as P

ITERS = 2
LANES = 128
SUB = 8

step_size = 0.5
weight_floor = 0.1
epsilon = 1e-06

RANK_BITS = (5, 2, 4, 1, 3, 0)
FIRST = 36


def owner_of_rank(owners):
    count = owners.bit_length() - 1
    bits = RANK_BITS if len(RANK_BITS) == count else range(count)
    first = FIRST % owners
    last = count - 1
    return [
        first ^ sum((rank >> (last - at) & 1) << (last - bit) for at, bit in enumerate(bits)) for rank in range(owners)
    ]


def lane_index(rows):
    return lax.broadcasted_iota(jnp.int32, (rows, LANES), 1)


def as_column(row):
    stations = row.shape[1]
    wide = jnp.broadcast_to(row, (stations, stations))
    at = lax.broadcasted_iota(jnp.int32, (stations, stations), 0)
    to = lax.broadcasted_iota(jnp.int32, (stations, stations), 1)
    return jnp.sum(jnp.where(at == to, wide, 0.0), axis=1, keepdims=True)


def in_lanes(columns):
    lane = lane_index(columns[0].shape[0])
    tile = jnp.zeros(lane.shape, jnp.float32)
    for at, column in enumerate(columns):
        tile = jnp.where(lane == at, column, tile)
    return tile


def lanes_of(chunk):
    return pl.ds(chunk * LANES, LANES)


def fold(values):
    row = lax.broadcasted_iota(jnp.int32, (SUB, LANES), 0)
    skewed = [values[-at % SUB] for at in range(SUB)]
    for shift in (1, 2, 4):
        moves = (row & shift) != 0
        skewed = [jnp.where(moves, skewed[(at - shift) % SUB], skewed[at]) for at in range(SUB)]
    terms = [skewed[0]] + [pltpu.roll(skewed[at], SUB - at, 0) for at in range(1, SUB)]
    return ((terms[0] + terms[1]) + (terms[2] + terms[3])) + ((terms[4] + terms[5]) + (terms[6] + terms[7]))


def store_tiles(owners, size, owner_rows, out):
    places = owner_of_rank(owners)
    group = SUB // math.gcd(SUB, size)
    tiles = group * size // SUB

    for step in range(owners // group):
        values = []
        for member in range(group):
            values += owner_rows(places[step * group + member])
        for tile in range(tiles):
            out[step * tiles + tile] = fold(values[tile * SUB : (tile + 1) * SUB])


def predict_kernel(
    rows, sens_hbm, model_hbm, observed_hbm, weight_hbm, scale, out, sens, model, observed, weight, sems
):
    halves, pieces = sens.shape[0] // SUB, sems.shape[0] - 3
    size = sens.shape[1] // pieces
    small = [
        pltpu.make_async_copy(source, target, sems.at[pieces + at])
        for at, (source, target) in enumerate(
            [(model_hbm, model), (observed_hbm, observed), (weight_hbm, weight)]
        )
    ]
    large = []
    for piece in range(pieces):
        lanes = pl.ds(piece * size, size)
        large.append(pltpu.make_async_copy(sens_hbm.at[:, lanes], sens.at[:, lanes], sems.at[piece]))
    small[0].start()
    for copy in large:
        copy.start()
    for copy in small[1:]:
        copy.start()
    small[0].wait()
    owners = size // LANES // rows

    def body(owner, acc):
        acc = list(acc)
        for row in range(rows):
            at = owner * rows + row
            value = model[pl.ds(at, 1), :]
            for half in range(halves):
                slot = (row % 4) * halves + half
                acc[slot] = acc[slot] + sens[half * SUB : (half + 1) * SUB, lanes_of(at)] * value
        return tuple(acc)

    acc = (jnp.zeros((SUB, LANES), jnp.float32),) * (4 * halves)
    for piece in range(pieces):
        large[piece].wait()
        for owner in range(piece * owners, (piece + 1) * owners):
            acc = body(owner, acc)
    total = [
        (acc[half] + acc[halves + half]) + (acc[2 * halves + half] + acc[3 * halves + half]) for half in range(halves)
    ]
    part = jnp.sum(jnp.concatenate(total, axis=0), axis=1, keepdims=True)
    for copy in small[1:]:
        copy.wait()
    column = as_column(weight[...])
    tile = in_lanes([part, column, as_column(observed[...]), scale[0] * column])
    for peer in range(out.shape[0]):
        out[peer] = tile


def residual_weights(predicted, station):
    weight, observed, scaled = station[:, 1:2], station[:, 2:3], station[:, 3:4]
    residual = weight * (predicted - observed)
    shape = (station.shape[0], LANES)
    return jnp.broadcast_to(weight * weight, shape), jnp.broadcast_to(scaled * residual, shape)


def first_terms_kernel(rows, owners, cell_blocks, root_cells, parts, sens, got, out, wide):
    halves = sens.shape[0] // SUB
    share = rows // 2
    core = lax.axis_index("phys")
    for place, method in enumerate((core, 1 - core)):
        station = parts[method * cell_blocks]
        total = station
        for block in range(1, cell_blocks):
            total = total + parts[method * cell_blocks + block]
        wide[place], wide[2 + place] = residual_weights(total[:, 0:1] / root_cells, station)

    def owner_rows(owner):
        columns, gradients = ([], []), []
        for row in range(share):
            lanes = lanes_of(owner * rows + core * share + row)
            gradient = None
            for method, source in enumerate((sens, got)):
                column = None
                for half in range(halves):
                    at = slice(half * SUB, (half + 1) * SUB)
                    block = source[at, lanes]
                    c = block * block * wide[method, at, :]
                    g = block * wide[2 + method, at, :]
                    column = c if column is None else column + c
                    gradient = g if gradient is None else gradient + g
                columns[method].append(column)
            gradients.append(gradient)
        return columns[0] + columns[1] + gradients

    store_tiles(owners, 3 * share, owner_rows, out)


def owner_sum_kernel(rows, owners, received, out):
    share = rows // 2
    core = lax.axis_index("phys")
    size = 3 * share
    sums = [jnp.sum(received[pl.ds(row, owners, stride=size), :], axis=0, keepdims=True) for row in range(size)]
    mine, other, gradient = sums[:share], sums[share : 2 * share], sums[2 * share :]
    columns = [jnp.where(core == 0, a, b) for a, b in zip(mine + other, other + mine)]
    largest = []
    for method in range(2):
        most = functools.reduce(jnp.maximum, columns[method * share : (method + 1) * share])
        largest.append(jnp.max(most, axis=1, keepdims=True))
    most = jnp.where(lane_index(1) < LANES // 2, largest[0], largest[1])
    fill = [jnp.zeros((out.shape[1] - size - 1, LANES), jnp.float32)] if out.shape[1] > size + 1 else []
    tile = jnp.concatenate(columns + gradient + [most] + fill, axis=0)
    for peer in range(out.shape[0]):
        out[peer] = tile


def message_kernel(rows, owners, cell_blocks, slices, out):
    size = 3 * (rows // 2) + 1
    core = lax.axis_index("phys")
    own = slices[core * cell_blocks + lax.axis_index("cell")]
    most = slices[0, size - 1 : size, :]
    for peer in range(1, slices.shape[0]):
        most = jnp.maximum(most, slices[peer, size - 1 : size, :])
    for row in range(size):
        value = own[row : row + 1] if row < size - 1 else most
        out[pl.ds(row, owners, stride=size), :] = jnp.broadcast_to(value, (owners, LANES))


def model_kernel(
    rows, owners, cell_blocks, physics, root_stations, message, slices, start, sens, got, out, own, model
):
    halves = sens.shape[0] // SUB
    share = rows // 2
    core = lax.axis_index("phys")
    position = lax.axis_index("sta")
    places = owner_of_rank(owners)
    size = message.shape[0] // owners
    most = jnp.max(message[pl.ds(size - 1, owners, stride=size), :], axis=0, keepdims=True)
    first_lanes = lane_index(1) < LANES // 2
    scales = []
    for inside in (first_lanes, ~first_lanes):
        largest = jnp.max(jnp.where(inside, most, 0.0), axis=1, keepdims=True)
        scales.append(1.0 / (largest + epsilon))

    def step(before, columns, summed):
        relative = None
        for column, scale in zip(columns, scales):
            r = jnp.sqrt(column * scale)
            relative = r if relative is None else relative + r
        weight = weight_floor + relative / physics
        return weight, before - step_size * (summed / (root_stations * weight))

    for rank, owner in enumerate(places):
        before = [start[owner * rows + half * share : owner * rows + (half + 1) * share, :] for half in range(2)]
        model[rank * share : (rank + 1) * share, :] = jnp.where(core == 0, before[0], before[1])
    for row in range(share):
        columns = [message[pl.ds(method * share + row, owners, stride=size), :] for method in range(2)]
        summed = message[pl.ds(2 * share + row, owners, stride=size), :]
        at = pl.ds(row, owners, stride=share)
        model[at, :] = step(model[at, :], columns, summed)[1]

    before = start[pl.ds(position * rows, rows), :]
    for half in range(2):
        place = half * cell_blocks + lax.axis_index("cell")
        columns = [slices[place, method * share : (method + 1) * share, :] for method in range(2)]
        summed = slices[place, 2 * share : 3 * share, :]
        at = slice(half * share, (half + 1) * share)
        own[0, at, :], own[1, at, :] = step(before[at], columns, summed)

    def body(rank, acc):
        acc = list(acc)
        for row in range(share):
            value = model[pl.ds(rank * share + row, 1), :]
            lanes = lanes_of(places[rank] * rows + core * share + row)
            for method, source in enumerate((sens, got)):
                for half in range(halves):
                    slot = ((row % 2) * 2 + method) * halves + half
                    acc[slot] = acc[slot] + source[half * SUB : (half + 1) * SUB, lanes] * value
        return tuple(acc)

    acc = (jnp.zeros((SUB, LANES), jnp.float32),) * (4 * halves)
    for rank in range(owners):
        acc = body(rank, acc)
    columns = []
    for method in range(2):
        total = [acc[method * halves + half] + acc[(2 + method) * halves + half] for half in range(halves)]
        columns.append(jnp.sum(jnp.concatenate(total, axis=0), axis=1, keepdims=True))
    lane = lane_index(columns[0].shape[0])
    tile = jnp.where(lane == core, columns[0], jnp.where(lane == 1 - core, columns[1], 0.0))
    for peer in range(out.shape[0]):
        out[peer] = tile


def second_terms_kernel(rows, owners, cell_blocks, root_cells, parts, stations, sens, got, out, wide):
    halves = sens.shape[0] // SUB
    core = lax.axis_index("phys")
    total = parts[0]
    for peer in range(1, parts.shape[0]):
        total = total + parts[peer]
    lane = lane_index(total.shape[0])
    for place, method in enumerate((core, 1 - core)):
        predicted = jnp.sum(jnp.where(lane == method, total, 0.0), axis=1, keepdims=True) / root_cells
        _, wide[place] = residual_weights(predicted, stations[method * cell_blocks])

    def owner_rows(owner):
        gradients = []
        for row in range(rows):
            lanes = lanes_of(owner * rows + row)
            gradient = None
            for method, source in enumerate((sens, got)):
                for half in range(halves):
                    at = slice(half * SUB, (half + 1) * SUB)
                    g = source[at, lanes] * wide[method, at, :]
                    gradient = g if gradient is None else gradient + g
            gradients.append(gradient)
        return gradients

    store_tiles(owners, rows, owner_rows, out)


def second_step_kernel(owners, root_stations, received, own, weight_out, gradient_out, model_out):
    rows = own.shape[1]
    for row in range(rows):
        total = jnp.sum(received[pl.ds(row, owners, stride=rows), :], axis=0, keepdims=True)
        weight = own[0, row : row + 1, :]
        gradient = total / (root_stations * weight)
        lanes = slice(row * LANES, (row + 1) * LANES)
        weight_out[:, lanes] = weight
        gradient_out[:, lanes] = gradient
        model_out[:, lanes] = own[1, row : row + 1, :] - step_size * gradient


def kernel_call(kernel, name, outs, operands, scratch=(), spaces=None, kept=True):
    make = pltpu.VMEM if kept else jax.ShapeDtypeStruct
    spaces = spaces or [pltpu.VMEM] * len(operands)
    operands = [
        pltpu.with_memory_space_constraint(x, space) if space == pltpu.HBM else x for x, space in zip(operands, spaces)
    ]
    return pl.pallas_call(
        kernel,
        name=name,
        out_shape=[make(shape, jnp.float32) for shape in outs],
        in_specs=[pl.BlockSpec(memory_space=space) for space in spaces],
        out_specs=[pl.BlockSpec(memory_space=pltpu.VMEM)] * len(outs),
        scratch_shapes=scratch,
        compiler_params=pltpu.CompilerParams(vmem_limit_bytes=16 * 2**20),
    )(*operands)


def per_device(sensitivity, observed, data_weight, phys_weight, start_model):
    owners = lax.axis_size("sta")
    cell_blocks = lax.axis_size("cell")
    physics = sensitivity.shape[0] * lax.axis_size("phys")
    stations, cell_count = sensitivity.shape[1:]
    chunks = cell_count // LANES
    rows = chunks // owners
    share = rows // 2
    root_cells = math.sqrt(cell_count * cell_blocks)
    root_stations = math.sqrt(stations * owners)
    sens = sensitivity.reshape(stations, cell_count)
    start = start_model.reshape(chunks, LANES)
    peers = physics * cell_blocks
    pieces = min(8, owners)

    def swap(array, axes, groups=None):
        return lax.all_to_all(array, axes, 0, 0, axis_index_groups=groups, tiled=True)

    def swap_rows(array):
        return swap(array.reshape(owners, 1, -1), "sta", [owner_of_rank(owners)]).reshape(-1, LANES)

    parts_shape = (peers, stations, LANES)
    first, sens = kernel_call(
        functools.partial(predict_kernel, rows),
        "predict",
        [parts_shape, (stations, cell_count)],
        [sens, start, observed, data_weight, phys_weight],
        scratch=[
            pltpu.VMEM((chunks, LANES), jnp.float32),
            pltpu.VMEM((1, stations), jnp.float32),
            pltpu.VMEM((1, stations), jnp.float32),
            pltpu.SemaphoreType.DMA((pieces + 3,)),
        ],
        spaces=[pltpu.HBM] * 4 + [pltpu.SMEM],
    )
    got = lax.ppermute(sens, "phys", [(0, 1), (1, 0)])
    first = swap(first, ("phys", "cell"))
    (terms,) = kernel_call(
        functools.partial(first_terms_kernel, rows, owners, cell_blocks, root_cells),
        "first_terms",
        [(owners * 3 * share // SUB, SUB, LANES)],
        [first, sens, got],
        scratch=[pltpu.VMEM((4, stations, LANES), jnp.float32)],
    )
    size = 3 * share + 1
    (slices,) = kernel_call(
        functools.partial(owner_sum_kernel, rows, owners),
        "owner_sum",
        [(peers, -(-size // SUB) * SUB, LANES)],
        [swap_rows(terms)],
    )
    slices = swap(slices, ("phys", "cell"))
    (message,) = kernel_call(
        functools.partial(message_kernel, rows, owners, cell_blocks),
        "message",
        [(owners * size, LANES)],
        [slices],
    )
    second, own = kernel_call(
        functools.partial(model_kernel, rows, owners, cell_blocks, physics, root_stations),
        "model",
        [parts_shape, (2, rows, LANES)],
        [swap_rows(message), slices, start, sens, got],
        scratch=[pltpu.VMEM((chunks // 2, LANES), jnp.float32)],
    )
    (terms,) = kernel_call(
        functools.partial(second_terms_kernel, rows, owners, cell_blocks, root_cells),
        "second_terms",
        [(chunks // SUB, SUB, LANES)],
        [swap(second, ("phys", "cell")), first, sens, got],
        scratch=[pltpu.VMEM((2, stations, LANES), jnp.float32)],
    )
    return tuple(
        kernel_call(
            functools.partial(second_step_kernel, owners, root_stations),
            "second_step",
            [(1, rows * LANES)] * 3,
            [swap_rows(terms), own],
            kept=False,
        )
    )


def solution(mesh):
    return jax.shard_map(
        per_device,
        mesh=mesh,
        in_specs=(
            P("phys", "sta", "cell"),
            P("phys", "sta"),
            P("phys", "sta"),
            P("phys"),
            P("cell"),
        ),
        out_specs=(P("cell", "sta"),) * 3,
        check_vma=False,
    )
```

```python
import functools
import math

import jax
import jax.numpy as jnp
from jax import lax
from jax.experimental import pallas as pl
from jax.experimental.pallas import tpu as pltpu
from jax.sharding import PartitionSpec as P

ITERS = 2
LANES = 128
SUB = 8

step_size = 0.5
weight_floor = 0.1
epsilon = 1e-06

RANK_BITS = (5, 2, 4, 1, 0, 3)
FIRST = 52


def owner_of_rank(owners):
    count = owners.bit_length() - 1
    bits = RANK_BITS if len(RANK_BITS) == count else range(count)
    first = FIRST % owners
    last = count - 1
    return [
        first ^ sum((rank >> (last - at) & 1) << (last - bit) for at, bit in enumerate(bits)) for rank in range(owners)
    ]


def lane_index(rows):
    return lax.broadcasted_iota(jnp.int32, (rows, LANES), 1)


def as_column(row):
    stations = row.shape[1]
    wide = jnp.broadcast_to(row, (stations, stations))
    at = lax.broadcasted_iota(jnp.int32, (stations, stations), 0)
    to = lax.broadcasted_iota(jnp.int32, (stations, stations), 1)
    return jnp.sum(jnp.where(at == to, wide, 0.0), axis=1, keepdims=True)


def in_lanes(columns):
    lane = lane_index(columns[0].shape[0])
    tile = jnp.zeros(lane.shape, jnp.float32)
    for at, column in enumerate(columns):
        tile = jnp.where(lane == at, column, tile)
    return tile


def lanes_of(chunk):
    return pl.ds(chunk * LANES, LANES)


def fold(values):
    row = lax.broadcasted_iota(jnp.int32, (SUB, LANES), 0)
    skewed = [values[-at % SUB] for at in range(SUB)]
    for shift in (1, 2, 4):
        moves = (row & shift) != 0
        skewed = [jnp.where(moves, skewed[(at - shift) % SUB], skewed[at]) for at in range(SUB)]
    terms = [skewed[0]] + [pltpu.roll(skewed[at], SUB - at, 0) for at in range(1, SUB)]
    return ((terms[0] + terms[1]) + (terms[2] + terms[3])) + ((terms[4] + terms[5]) + (terms[6] + terms[7]))


def store_tiles(owners, size, owner_rows, out):
    places = owner_of_rank(owners)
    group = SUB // math.gcd(SUB, size)
    tiles = group * size // SUB

    for step in range(owners // group):
        values = []
        for member in range(group):
            values += owner_rows(places[step * group + member])
        for tile in range(tiles):
            out[step * tiles + tile] = fold(values[tile * SUB : (tile + 1) * SUB])


def predict_kernel(
    rows, sens_hbm, model_hbm, observed_hbm, weight_hbm, scale, out, sens, model, observed, weight, sems
):
    halves, pieces = sens.shape[0] // SUB, sems.shape[0] - 3
    size = sens.shape[1] // pieces
    small = [
        pltpu.make_async_copy(source, target, sems.at[pieces + at])
        for at, (source, target) in enumerate(
            [(model_hbm, model), (observed_hbm, observed), (weight_hbm, weight)]
        )
    ]
    large = []
    for piece in range(pieces):
        lanes = pl.ds(piece * size, size)
        large.append(pltpu.make_async_copy(sens_hbm.at[:, lanes], sens.at[:, lanes], sems.at[piece]))
    small[0].start()
    for copy in large:
        copy.start()
    for copy in small[1:]:
        copy.start()
    small[0].wait()
    owners = size // LANES // rows

    def body(owner, acc):
        acc = list(acc)
        for row in range(rows):
            at = owner * rows + row
            value = model[pl.ds(at, 1), :]
            for half in range(halves):
                slot = (row % 4) * halves + half
                acc[slot] = acc[slot] + sens[half * SUB : (half + 1) * SUB, lanes_of(at)] * value
        return tuple(acc)

    acc = (jnp.zeros((SUB, LANES), jnp.float32),) * (4 * halves)
    for piece in range(pieces):
        large[piece].wait()
        for owner in range(piece * owners, (piece + 1) * owners):
            acc = body(owner, acc)
    total = [
        (acc[half] + acc[halves + half]) + (acc[2 * halves + half] + acc[3 * halves + half]) for half in range(halves)
    ]
    part = jnp.sum(jnp.concatenate(total, axis=0), axis=1, keepdims=True)
    for copy in small[1:]:
        copy.wait()
    column = as_column(weight[...])
    tile = in_lanes([part, column, as_column(observed[...]), scale[0] * column])
    for peer in range(out.shape[0]):
        out[peer] = tile


def residual_weights(predicted, station):
    weight, observed, scaled = station[:, 1:2], station[:, 2:3], station[:, 3:4]
    residual = weight * (predicted - observed)
    shape = (station.shape[0], LANES)
    return jnp.broadcast_to(weight * weight, shape), jnp.broadcast_to(scaled * residual, shape)


def first_terms_kernel(rows, owners, cell_blocks, root_cells, parts, sens, got, out, wide):
    halves = sens.shape[0] // SUB
    share = rows // 2
    core = lax.axis_index("phys")
    for place, method in enumerate((core, 1 - core)):
        station = parts[method * cell_blocks]
        total = station
        for block in range(1, cell_blocks):
            total = total + parts[method * cell_blocks + block]
        wide[place], wide[2 + place] = residual_weights(total[:, 0:1] / root_cells, station)

    def owner_rows(owner):
        columns, gradients = ([], []), []
        for row in range(share):
            lanes = lanes_of(owner * rows + core * share + row)
            gradient = None
            for method, source in enumerate((sens, got)):
                column = None
                for half in range(halves):
                    at = slice(half * SUB, (half + 1) * SUB)
                    block = source[at, lanes]
                    c = block * block * wide[method, at, :]
                    g = block * wide[2 + method, at, :]
                    column = c if column is None else column + c
                    gradient = g if gradient is None else gradient + g
                columns[method].append(column)
            gradients.append(gradient)
        return columns[0] + columns[1] + gradients

    store_tiles(owners, 3 * share, owner_rows, out)


def owner_sum_kernel(rows, owners, received, out):
    share = rows // 2
    core = lax.axis_index("phys")
    size = 3 * share
    sums = [jnp.sum(received[pl.ds(row, owners, stride=size), :], axis=0, keepdims=True) for row in range(size)]
    mine, other, gradient = sums[:share], sums[share : 2 * share], sums[2 * share :]
    columns = [jnp.where(core == 0, a, b) for a, b in zip(mine + other, other + mine)]
    largest = []
    for method in range(2):
        most = functools.reduce(jnp.maximum, columns[method * share : (method + 1) * share])
        largest.append(jnp.max(most, axis=1, keepdims=True))
    most = jnp.where(lane_index(1) < LANES // 2, largest[0], largest[1])
    fill = [jnp.zeros((out.shape[1] - size - 1, LANES), jnp.float32)] if out.shape[1] > size + 1 else []
    tile = jnp.concatenate(columns + gradient + [most] + fill, axis=0)
    for peer in range(out.shape[0]):
        out[peer] = tile


def message_kernel(rows, owners, cell_blocks, slices, out):
    size = 3 * (rows // 2) + 1
    core = lax.axis_index("phys")
    own = slices[core * cell_blocks + lax.axis_index("cell")]
    most = slices[0, size - 1 : size, :]
    for peer in range(1, slices.shape[0]):
        most = jnp.maximum(most, slices[peer, size - 1 : size, :])
    for row in range(size):
        value = own[row : row + 1] if row < size - 1 else most
        out[pl.ds(row, owners, stride=size), :] = jnp.broadcast_to(value, (owners, LANES))


def model_kernel(
    rows, owners, cell_blocks, physics, root_stations, message, slices, start, sens, got, out, own, model
):
    halves = sens.shape[0] // SUB
    share = rows // 2
    core = lax.axis_index("phys")
    position = lax.axis_index("sta")
    places = owner_of_rank(owners)
    size = message.shape[0] // owners
    most = jnp.max(message[pl.ds(size - 1, owners, stride=size), :], axis=0, keepdims=True)
    first_lanes = lane_index(1) < LANES // 2
    scales = []
    for inside in (first_lanes, ~first_lanes):
        largest = jnp.max(jnp.where(inside, most, 0.0), axis=1, keepdims=True)
        scales.append(1.0 / (largest + epsilon))

    def step(before, columns, summed):
        relative = None
        for column, scale in zip(columns, scales):
            r = jnp.sqrt(column * scale)
            relative = r if relative is None else relative + r
        weight = weight_floor + relative / physics
        return weight, before - step_size * (summed / (root_stations * weight))

    for rank, owner in enumerate(places):
        before = [start[owner * rows + half * share : owner * rows + (half + 1) * share, :] for half in range(2)]
        model[rank * share : (rank + 1) * share, :] = jnp.where(core == 0, before[0], before[1])
    for row in range(share):
        columns = [message[pl.ds(method * share + row, owners, stride=size), :] for method in range(2)]
        summed = message[pl.ds(2 * share + row, owners, stride=size), :]
        at = pl.ds(row, owners, stride=share)
        model[at, :] = step(model[at, :], columns, summed)[1]

    before = start[pl.ds(position * rows, rows), :]
    for half in range(2):
        place = half * cell_blocks + lax.axis_index("cell")
        columns = [slices[place, method * share : (method + 1) * share, :] for method in range(2)]
        summed = slices[place, 2 * share : 3 * share, :]
        at = slice(half * share, (half + 1) * share)
        own[0, at, :], own[1, at, :] = step(before[at], columns, summed)

    def body(rank, acc):
        acc = list(acc)
        for row in range(share):
            value = model[pl.ds(rank * share + row, 1), :]
            lanes = lanes_of(places[rank] * rows + core * share + row)
            for method, source in enumerate((sens, got)):
                for half in range(halves):
                    slot = ((row % 2) * 2 + method) * halves + half
                    acc[slot] = acc[slot] + source[half * SUB : (half + 1) * SUB, lanes] * value
        return tuple(acc)

    acc = (jnp.zeros((SUB, LANES), jnp.float32),) * (4 * halves)
    for rank in range(owners):
        acc = body(rank, acc)
    columns = []
    for method in range(2):
        total = [acc[method * halves + half] + acc[(2 + method) * halves + half] for half in range(halves)]
        columns.append(jnp.sum(jnp.concatenate(total, axis=0), axis=1, keepdims=True))
    lane = lane_index(columns[0].shape[0])
    tile = jnp.where(lane == core, columns[0], jnp.where(lane == 1 - core, columns[1], 0.0))
    for peer in range(out.shape[0]):
        out[peer] = tile


def second_terms_kernel(rows, owners, cell_blocks, root_cells, parts, stations, sens, got, out, wide):
    halves = sens.shape[0] // SUB
    core = lax.axis_index("phys")
    total = parts[0]
    for peer in range(1, parts.shape[0]):
        total = total + parts[peer]
    lane = lane_index(total.shape[0])
    for place, method in enumerate((core, 1 - core)):
        predicted = jnp.sum(jnp.where(lane == method, total, 0.0), axis=1, keepdims=True) / root_cells
        _, wide[place] = residual_weights(predicted, stations[method * cell_blocks])

    def owner_rows(owner):
        gradients = []
        for row in range(rows):
            lanes = lanes_of(owner * rows + row)
            gradient = None
            for method, source in enumerate((sens, got)):
                for half in range(halves):
                    at = slice(half * SUB, (half + 1) * SUB)
                    g = source[at, lanes] * wide[method, at, :]
                    gradient = g if gradient is None else gradient + g
            gradients.append(gradient)
        return gradients

    store_tiles(owners, rows, owner_rows, out)


def second_step_kernel(owners, root_stations, received, own, weight_out, gradient_out, model_out):
    rows = own.shape[1]
    for row in range(rows):
        total = jnp.sum(received[pl.ds(row, owners, stride=rows), :], axis=0, keepdims=True)
        weight = own[0, row : row + 1, :]
        gradient = total / (root_stations * weight)
        lanes = slice(row * LANES, (row + 1) * LANES)
        weight_out[:, lanes] = weight
        gradient_out[:, lanes] = gradient
        model_out[:, lanes] = own[1, row : row + 1, :] - step_size * gradient


def kernel_call(kernel, name, outs, operands, scratch=(), spaces=None, kept=True):
    make = pltpu.VMEM if kept else jax.ShapeDtypeStruct
    spaces = spaces or [pltpu.VMEM] * len(operands)
    operands = [
        pltpu.with_memory_space_constraint(x, space) if space == pltpu.HBM else x for x, space in zip(operands, spaces)
    ]
    return pl.pallas_call(
        kernel,
        name=name,
        out_shape=[make(shape, jnp.float32) for shape in outs],
        in_specs=[pl.BlockSpec(memory_space=space) for space in spaces],
        out_specs=[pl.BlockSpec(memory_space=pltpu.VMEM)] * len(outs),
        scratch_shapes=scratch,
        compiler_params=pltpu.CompilerParams(vmem_limit_bytes=16 * 2**20),
    )(*operands)


def per_device(sensitivity, observed, data_weight, phys_weight, start_model):
    owners = lax.axis_size("sta")
    cell_blocks = lax.axis_size("cell")
    physics = sensitivity.shape[0] * lax.axis_size("phys")
    stations, cell_count = sensitivity.shape[1:]
    chunks = cell_count // LANES
    rows = chunks // owners
    share = rows // 2
    root_cells = math.sqrt(cell_count * cell_blocks)
    root_stations = math.sqrt(stations * owners)
    sens = sensitivity.reshape(stations, cell_count)
    start = start_model.reshape(chunks, LANES)
    peers = physics * cell_blocks
    pieces = min(8, owners)

    def swap(array, axes, groups=None):
        return lax.all_to_all(array, axes, 0, 0, axis_index_groups=groups, tiled=True)

    def swap_rows(array):
        return swap(array.reshape(owners, 1, -1), "sta", [owner_of_rank(owners)]).reshape(-1, LANES)

    parts_shape = (peers, stations, LANES)
    first, sens = kernel_call(
        functools.partial(predict_kernel, rows),
        "predict",
        [parts_shape, (stations, cell_count)],
        [sens, start, observed, data_weight, phys_weight],
        scratch=[
            pltpu.VMEM((chunks, LANES), jnp.float32),
            pltpu.VMEM((1, stations), jnp.float32),
            pltpu.VMEM((1, stations), jnp.float32),
            pltpu.SemaphoreType.DMA((pieces + 3,)),
        ],
        spaces=[pltpu.HBM] * 4 + [pltpu.SMEM],
    )
    got = lax.ppermute(sens, "phys", [(0, 1), (1, 0)])
    first = swap(first, ("phys", "cell"))
    (terms,) = kernel_call(
        functools.partial(first_terms_kernel, rows, owners, cell_blocks, root_cells),
        "first_terms",
        [(owners * 3 * share // SUB, SUB, LANES)],
        [first, sens, got],
        scratch=[pltpu.VMEM((4, stations, LANES), jnp.float32)],
    )
    size = 3 * share + 1
    (slices,) = kernel_call(
        functools.partial(owner_sum_kernel, rows, owners),
        "owner_sum",
        [(peers, -(-size // SUB) * SUB, LANES)],
        [swap_rows(terms)],
    )
    slices = swap(slices, ("phys", "cell"))
    (message,) = kernel_call(
        functools.partial(message_kernel, rows, owners, cell_blocks),
        "message",
        [(owners * size, LANES)],
        [slices],
    )
    second, own = kernel_call(
        functools.partial(model_kernel, rows, owners, cell_blocks, physics, root_stations),
        "model",
        [parts_shape, (2, rows, LANES)],
        [swap_rows(message), slices, start, sens, got],
        scratch=[pltpu.VMEM((chunks // 2, LANES), jnp.float32)],
    )
    (terms,) = kernel_call(
        functools.partial(second_terms_kernel, rows, owners, cell_blocks, root_cells),
        "second_terms",
        [(chunks // SUB, SUB, LANES)],
        [swap(second, ("phys", "cell")), first, sens, got],
        scratch=[pltpu.VMEM((2, stations, LANES), jnp.float32)],
    )
    return tuple(
        kernel_call(
            functools.partial(second_step_kernel, owners, root_stations),
            "second_step",
            [(1, rows * LANES)] * 3,
            [swap_rows(terms), own],
            kept=False,
        )
    )


def solution(mesh):
    return jax.shard_map(
        per_device,
        mesh=mesh,
        in_specs=(
            P("phys", "sta", "cell"),
            P("phys", "sta"),
            P("phys", "sta"),
            P("phys"),
            P("cell"),
        ),
        out_specs=(P("cell", "sta"),) * 3,
        check_vma=False,
    )
```

```python
import functools
import math

import jax
import jax.numpy as jnp
from jax import lax
from jax.experimental import pallas as pl
from jax.experimental.pallas import tpu as pltpu
from jax.sharding import PartitionSpec as P

ITERS = 2
LANES = 128
SUB = 8

step_size = 0.5
weight_floor = 0.1
epsilon = 1e-06

RANK_BITS = (5, 2, 4, 1, 0, 3)
FIRST = 52


def owner_of_rank(owners):
    count = owners.bit_length() - 1
    bits = RANK_BITS if len(RANK_BITS) == count else range(count)
    first = FIRST % owners
    last = count - 1
    return [
        first ^ sum((rank >> (last - at) & 1) << (last - bit) for at, bit in enumerate(bits)) for rank in range(owners)
    ]


def lane_index(rows):
    return lax.broadcasted_iota(jnp.int32, (rows, LANES), 1)


def as_column(row):
    stations = row.shape[1]
    wide = jnp.broadcast_to(row, (stations, stations))
    at = lax.broadcasted_iota(jnp.int32, (stations, stations), 0)
    to = lax.broadcasted_iota(jnp.int32, (stations, stations), 1)
    return jnp.sum(jnp.where(at == to, wide, 0.0), axis=1, keepdims=True)


def in_lanes(columns):
    lane = lane_index(columns[0].shape[0])
    tile = jnp.zeros(lane.shape, jnp.float32)
    for at, column in enumerate(columns):
        tile = jnp.where(lane == at, column, tile)
    return tile


def lanes_of(chunk):
    return pl.ds(chunk * LANES, LANES)


def fold(values):
    row = lax.broadcasted_iota(jnp.int32, (SUB, LANES), 0)
    skewed = [values[-at % SUB] for at in range(SUB)]
    for shift in (1, 2, 4):
        moves = (row & shift) != 0
        skewed = [jnp.where(moves, skewed[(at - shift) % SUB], skewed[at]) for at in range(SUB)]
    terms = [skewed[0]] + [pltpu.roll(skewed[at], SUB - at, 0) for at in range(1, SUB)]
    return ((terms[0] + terms[1]) + (terms[2] + terms[3])) + ((terms[4] + terms[5]) + (terms[6] + terms[7]))


def store_tiles(owners, size, owner_rows, out):
    places = owner_of_rank(owners)
    group = SUB // math.gcd(SUB, size)
    tiles = group * size // SUB

    for step in range(owners // group):
        values = []
        for member in range(group):
            values += owner_rows(places[step * group + member])
        for tile in range(tiles):
            out[step * tiles + tile] = fold(values[tile * SUB : (tile + 1) * SUB])


def predict_kernel(
    rows, sens_hbm, model_hbm, observed_hbm, weight_hbm, scale, out, sens, model, observed, weight, sems
):
    halves, pieces = sens.shape[0] // SUB, sems.shape[0] - 3
    size = sens.shape[1] // pieces
    small = [
        pltpu.make_async_copy(source, target, sems.at[pieces + at])
        for at, (source, target) in enumerate(
            [(model_hbm, model), (observed_hbm, observed), (weight_hbm, weight)]
        )
    ]
    large = []
    for piece in range(pieces):
        lanes = pl.ds(piece * size, size)
        large.append(pltpu.make_async_copy(sens_hbm.at[:, lanes], sens.at[:, lanes], sems.at[piece]))
    small[0].start()
    for copy in large:
        copy.start()
    for copy in small[1:]:
        copy.start()
    small[0].wait()
    owners = size // LANES // rows

    def body(owner, acc):
        acc = list(acc)
        for row in range(rows):
            at = owner * rows + row
            value = model[pl.ds(at, 1), :]
            for half in range(halves):
                slot = (row % 4) * halves + half
                acc[slot] = acc[slot] + sens[half * SUB : (half + 1) * SUB, lanes_of(at)] * value
        return tuple(acc)

    acc = (jnp.zeros((SUB, LANES), jnp.float32),) * (4 * halves)
    for piece in range(pieces):
        large[piece].wait()
        for owner in range(piece * owners, (piece + 1) * owners):
            acc = body(owner, acc)
    total = [
        (acc[half] + acc[halves + half]) + (acc[2 * halves + half] + acc[3 * halves + half]) for half in range(halves)
    ]
    part = jnp.sum(jnp.concatenate(total, axis=0), axis=1, keepdims=True)
    for copy in small[1:]:
        copy.wait()
    column = as_column(weight[...])
    tile = in_lanes([part, column, as_column(observed[...]), scale[0] * column])
    for peer in range(out.shape[0]):
        out[peer] = tile


def residual_weights(predicted, station):
    weight, observed, scaled = station[:, 1:2], station[:, 2:3], station[:, 3:4]
    residual = weight * (predicted - observed)
    shape = (station.shape[0], LANES)
    return jnp.broadcast_to(weight * weight, shape), jnp.broadcast_to(scaled * residual, shape)


def first_terms_kernel(rows, owners, cell_blocks, root_cells, parts, sens, got, out, wide):
    halves = sens.shape[0] // SUB
    share = rows // 2
    core = lax.axis_index("phys")
    for slot, method in enumerate((core, 1 - core)):
        place = (1 - method) * cell_blocks
        station = parts[place]
        total = station
        for block in range(1, cell_blocks):
            total = total + parts[place + block]
        wide[slot], wide[2 + slot] = residual_weights(total[:, 0:1] / root_cells, station)

    def owner_rows(owner):
        columns, gradients = ([], []), []
        for row in range(share):
            lanes = lanes_of(owner * rows + core * share + row)
            gradient = None
            for method, source in enumerate((sens, got)):
                column = None
                for half in range(halves):
                    at = slice(half * SUB, (half + 1) * SUB)
                    block = source[at, lanes]
                    c = block * block * wide[method, at, :]
                    g = block * wide[2 + method, at, :]
                    column = c if column is None else column + c
                    gradient = g if gradient is None else gradient + g
                columns[method].append(column)
            gradients.append(gradient)
        return columns[0] + columns[1] + gradients

    store_tiles(owners, 3 * share, owner_rows, out)


def owner_sum_kernel(rows, owners, received, out):
    share = rows // 2
    core = lax.axis_index("phys")
    size = 3 * share
    sums = [jnp.sum(received[pl.ds(row, owners, stride=size), :], axis=0, keepdims=True) for row in range(size)]
    mine, other, gradient = sums[:share], sums[share : 2 * share], sums[2 * share :]
    columns = [jnp.where(core == 0, a, b) for a, b in zip(mine + other, other + mine)]
    largest = []
    for method in range(2):
        most = functools.reduce(jnp.maximum, columns[method * share : (method + 1) * share])
        largest.append(jnp.max(most, axis=1, keepdims=True))
    most = jnp.where(lane_index(1) < LANES // 2, largest[0], largest[1])
    fill = [jnp.zeros((out.shape[1] - size - 1, LANES), jnp.float32)] if out.shape[1] > size + 1 else []
    tile = jnp.concatenate(columns + gradient + [most] + fill, axis=0)
    for peer in range(out.shape[0]):
        out[peer] = tile


def message_kernel(rows, owners, cell_blocks, slices, out):
    size = 3 * (rows // 2) + 1
    core = lax.axis_index("phys")
    own = slices[core * cell_blocks + lax.axis_index("cell")]
    most = slices[0, size - 1 : size, :]
    for peer in range(1, slices.shape[0]):
        most = jnp.maximum(most, slices[peer, size - 1 : size, :])
    for row in range(size):
        value = own[row : row + 1] if row < size - 1 else most
        out[pl.ds(row, owners, stride=size), :] = jnp.broadcast_to(value, (owners, LANES))


def model_kernel(
    rows, owners, cell_blocks, physics, root_stations, message, slices, start, sens, got, out, own, model
):
    halves = sens.shape[0] // SUB
    share = rows // 2
    core = lax.axis_index("phys")
    position = lax.axis_index("sta")
    places = owner_of_rank(owners)
    size = message.shape[0] // owners
    most = jnp.max(message[pl.ds(size - 1, owners, stride=size), :], axis=0, keepdims=True)
    first_lanes = lane_index(1) < LANES // 2
    scales = []
    for inside in (first_lanes, ~first_lanes):
        largest = jnp.max(jnp.where(inside, most, 0.0), axis=1, keepdims=True)
        scales.append(1.0 / (largest + epsilon))

    def step(before, columns, summed):
        relative = None
        for column, scale in zip(columns, scales):
            r = jnp.sqrt(column * scale)
            relative = r if relative is None else relative + r
        weight = weight_floor + relative / physics
        return weight, before - step_size * (summed / (root_stations * weight))

    for rank, owner in enumerate(places):
        before = [start[owner * rows + half * share : owner * rows + (half + 1) * share, :] for half in range(2)]
        model[rank * share : (rank + 1) * share, :] = jnp.where(core == 0, before[0], before[1])
    for row in range(share):
        columns = [message[pl.ds(method * share + row, owners, stride=size), :] for method in range(2)]
        summed = message[pl.ds(2 * share + row, owners, stride=size), :]
        at = pl.ds(row, owners, stride=share)
        model[at, :] = step(model[at, :], columns, summed)[1]

    before = start[pl.ds(position * rows, rows), :]
    for half in range(2):
        place = half * cell_blocks + lax.axis_index("cell")
        columns = [slices[place, method * share : (method + 1) * share, :] for method in range(2)]
        summed = slices[place, 2 * share : 3 * share, :]
        at = slice(half * share, (half + 1) * share)
        own[0, at, :], own[1, at, :] = step(before[at], columns, summed)

    def body(rank, acc):
        acc = list(acc)
        for row in range(share):
            value = model[pl.ds(rank * share + row, 1), :]
            lanes = lanes_of(places[rank] * rows + core * share + row)
            for method, source in enumerate((sens, got)):
                for half in range(halves):
                    slot = ((row % 2) * 2 + method) * halves + half
                    acc[slot] = acc[slot] + source[half * SUB : (half + 1) * SUB, lanes] * value
        return tuple(acc)

    acc = (jnp.zeros((SUB, LANES), jnp.float32),) * (4 * halves)
    for rank in range(owners):
        acc = body(rank, acc)
    columns = []
    for method in range(2):
        total = [acc[method * halves + half] + acc[(2 + method) * halves + half] for half in range(halves)]
        columns.append(jnp.sum(jnp.concatenate(total, axis=0), axis=1, keepdims=True))
    lane = lane_index(columns[0].shape[0])
    tile = jnp.where(lane == core, columns[0], jnp.where(lane == 1 - core, columns[1], 0.0))
    for peer in range(out.shape[0]):
        out[peer] = tile


def second_terms_kernel(rows, owners, cell_blocks, root_cells, parts, stations, sens, got, out, wide):
    halves = sens.shape[0] // SUB
    core = lax.axis_index("phys")
    total = parts[0]
    for peer in range(1, parts.shape[0]):
        total = total + parts[peer]
    lane = lane_index(total.shape[0])
    for place, method in enumerate((core, 1 - core)):
        predicted = jnp.sum(jnp.where(lane == method, total, 0.0), axis=1, keepdims=True) / root_cells
        _, wide[place] = residual_weights(predicted, stations[(1 - method) * cell_blocks])

    def owner_rows(owner):
        gradients = []
        for row in range(rows):
            lanes = lanes_of(owner * rows + row)
            gradient = None
            for method, source in enumerate((sens, got)):
                for half in range(halves):
                    at = slice(half * SUB, (half + 1) * SUB)
                    g = source[at, lanes] * wide[method, at, :]
                    gradient = g if gradient is None else gradient + g
            gradients.append(gradient)
        return gradients

    store_tiles(owners, rows, owner_rows, out)


def second_step_kernel(owners, root_stations, received, own, weight_out, gradient_out, model_out):
    rows = own.shape[1]
    for row in range(rows):
        total = jnp.sum(received[pl.ds(row, owners, stride=rows), :], axis=0, keepdims=True)
        weight = own[0, row : row + 1, :]
        gradient = total / (root_stations * weight)
        lanes = slice(row * LANES, (row + 1) * LANES)
        weight_out[:, lanes] = weight
        gradient_out[:, lanes] = gradient
        model_out[:, lanes] = own[1, row : row + 1, :] - step_size * gradient


def kernel_call(kernel, name, outs, operands, scratch=(), spaces=None, kept=True):
    make = pltpu.VMEM if kept else jax.ShapeDtypeStruct
    spaces = spaces or [pltpu.VMEM] * len(operands)
    operands = [
        pltpu.with_memory_space_constraint(x, space) if space == pltpu.HBM else x for x, space in zip(operands, spaces)
    ]
    return pl.pallas_call(
        kernel,
        name=name,
        out_shape=[make(shape, jnp.float32) for shape in outs],
        in_specs=[pl.BlockSpec(memory_space=space) for space in spaces],
        out_specs=[pl.BlockSpec(memory_space=pltpu.VMEM)] * len(outs),
        scratch_shapes=scratch,
        compiler_params=pltpu.CompilerParams(vmem_limit_bytes=16 * 2**20),
    )(*operands)


def per_device(sensitivity, observed, data_weight, phys_weight, start_model):
    owners = lax.axis_size("sta")
    cell_blocks = lax.axis_size("cell")
    physics = sensitivity.shape[0] * lax.axis_size("phys")
    stations, cell_count = sensitivity.shape[1:]
    chunks = cell_count // LANES
    rows = chunks // owners
    share = rows // 2
    root_cells = math.sqrt(cell_count * cell_blocks)
    root_stations = math.sqrt(stations * owners)
    sens = sensitivity.reshape(stations, cell_count)
    start = start_model.reshape(chunks, LANES)
    peers = physics * cell_blocks
    pieces = min(8, owners)

    def swap(array, axes, groups=None):
        return lax.all_to_all(array, axes, 0, 0, axis_index_groups=groups, tiled=True)

    def swap_rows(array):
        return swap(array.reshape(owners, 1, -1), "sta", [owner_of_rank(owners)]).reshape(-1, LANES)

    parts_shape = (peers, stations, LANES)
    first, sens = kernel_call(
        functools.partial(predict_kernel, rows),
        "predict",
        [parts_shape, (stations, cell_count)],
        [sens, start, observed, data_weight, phys_weight],
        scratch=[
            pltpu.VMEM((chunks, LANES), jnp.float32),
            pltpu.VMEM((1, stations), jnp.float32),
            pltpu.VMEM((1, stations), jnp.float32),
            pltpu.SemaphoreType.DMA((pieces + 3,)),
        ],
        spaces=[pltpu.HBM] * 4 + [pltpu.SMEM],
    )
    got = lax.ppermute(sens, "phys", [(0, 1), (1, 0)])
    late_first = [[*range(cell_blocks, peers), *range(cell_blocks)]]
    first = swap(first, ("phys", "cell"), late_first)
    (terms,) = kernel_call(
        functools.partial(first_terms_kernel, rows, owners, cell_blocks, root_cells),
        "first_terms",
        [(owners * 3 * share // SUB, SUB, LANES)],
        [first, sens, got],
        scratch=[pltpu.VMEM((4, stations, LANES), jnp.float32)],
    )
    size = 3 * share + 1
    (slices,) = kernel_call(
        functools.partial(owner_sum_kernel, rows, owners),
        "owner_sum",
        [(peers, -(-size // SUB) * SUB, LANES)],
        [swap_rows(terms)],
    )
    slices = swap(slices, ("phys", "cell"))
    (message,) = kernel_call(
        functools.partial(message_kernel, rows, owners, cell_blocks),
        "message",
        [(owners * size, LANES)],
        [slices],
    )
    second, own = kernel_call(
        functools.partial(model_kernel, rows, owners, cell_blocks, physics, root_stations),
        "model",
        [parts_shape, (2, rows, LANES)],
        [swap_rows(message), slices, start, sens, got],
        scratch=[pltpu.VMEM((chunks // 2, LANES), jnp.float32)],
    )
    (terms,) = kernel_call(
        functools.partial(second_terms_kernel, rows, owners, cell_blocks, root_cells),
        "second_terms",
        [(chunks // SUB, SUB, LANES)],
        [swap(second, ("phys", "cell")), first, sens, got],
        scratch=[pltpu.VMEM((2, stations, LANES), jnp.float32)],
    )
    return tuple(
        kernel_call(
            functools.partial(second_step_kernel, owners, root_stations),
            "second_step",
            [(1, rows * LANES)] * 3,
            [swap_rows(terms), own],
            kept=False,
        )
    )


def solution(mesh):
    return jax.shard_map(
        per_device,
        mesh=mesh,
        in_specs=(
            P("phys", "sta", "cell"),
            P("phys", "sta"),
            P("phys", "sta"),
            P("phys"),
            P("cell"),
        ),
        out_specs=(P("cell", "sta"),) * 3,
        check_vma=False,
    )
```
